512 devices in a mesh: region: 16 (over y, core), local: 32 (over z, x).
Axes of the slice: x: 4, y: 8, z: 8, core: 2. Of those that a mesh axis runs over, the one named last changes fastest.
Arguments:
- positions: float32 [32768, 4, 256], P(('region', 'local')), as said below
- pair_list: int32 [32768, 2], P(('region', 'local')), may hold values from 0 to 639, as said below
- pair_count: int32 [512], P(('region', 'local')), may hold values from 16 to 64, as said below
- active: int32 [32768], P(('region', 'local')), may hold values 0 or 1
Outputs:
- accel: float32 [32768, 3, 256], P(('region', 'local'))
The draws below stay inside these ranges and needn't reach their ends.
Inputs may be any that keep to these rules, and one draw needn't show every extreme that they name: `pair_list`: column 0 lies in 0 to 63 and column 1 in 0 to 639; no slot pairs a leaf with itself. `pair_count`: whole region groups carry the full 64 live slots on every device, two to four times the count of other groups' devices. `positions`: masses are positive.
All inputs are finite; a program needn't handle non-finite values. No bound on the sum of `active` on one device may be relied on, other than what follows from the above.
Results may differ from the reference program's by a relative error of at most 0.0003.
Values sent between devices are 32-bit elements; how exact they have to be, the bound alone decides.
A program may use at most 64 MiB of HBM per device.

```python
import math
import jax
import jax.numpy as jnp
from jax import lax

LEAF = 256
LEAF_DEV = 64
PAIR_DEV = 64
LOCAL_LEAVES = 2048
LEAVES = 32768
PAIRS = 32768
N_REGION = 16
N_LOCAL = 32
DEVICES = 512


def draw_positions(key, part):
    key = jax.random.fold_in(key, 11)
    keys = jax.random.split(key, 3)
    centre = 0.7 * jax.random.normal(keys[0], (LEAVES, 3, 1), jnp.float32)
    offset = 0.6 * jax.random.normal(keys[1], (LEAVES, 3, LEAF), jnp.float32)
    mass = jnp.exp(jax.random.uniform(keys[2], (LEAVES, 1, LEAF), jnp.float32, -0.7, 0.7)) / LEAF
    return jnp.concatenate([centre + offset, mass], axis=1)


def draw_pair_list(key, part):
    key = jax.random.fold_in(key, 23)
    keys = jax.random.split(key, 3)
    rows = jnp.arange(PAIRS, dtype=jnp.int32)
    owner = jax.random.randint(keys[0], (PAIRS,), 0, LEAF_DEV, jnp.int32)
    leaf = jax.random.randint(keys[1], (PAIRS,), 0, LEAF_DEV, jnp.int32)
    turn = jax.random.randint(keys[2], (DEVICES,), 0, 10, jnp.int32)
    shard = (rows % PAIR_DEV + turn[rows // PAIR_DEV]) % 10
    same = (shard == 2) & (leaf == owner)
    leaf = jnp.where(same, (leaf + 1) % LEAF_DEV, leaf)
    partner = shard * LEAF_DEV + leaf
    return jnp.stack([owner, partner], axis=1).astype(jnp.int32)


def draw_pair_count(key, part):
    key = jax.random.fold_in(key, 37)
    keys = jax.random.split(key, 3)
    groups = DEVICES // (LOCAL_LEAVES // LEAF_DEV)
    heavy = jax.random.randint(keys[0], (groups,), 0, 8, jnp.int32) == 0
    forced = jax.random.randint(keys[1], (), 0, groups, jnp.int32)
    heavy = heavy | (jnp.arange(groups, dtype=jnp.int32) == forced)
    light = jax.random.randint(keys[2], (DEVICES,), PAIR_DEV // 4, PAIR_DEV // 2 + 1, jnp.int32)
    group_of = jnp.arange(DEVICES, dtype=jnp.int32) // (LOCAL_LEAVES // LEAF_DEV)
    return jnp.where(heavy[group_of], PAIR_DEV, light).astype(jnp.int32)


def set_ends(result, key, least, largest):
    extent = result.shape
    spot = [jax.random.randint(jax.random.fold_in(key, axis), (), 0, extent[axis]) for axis in range(len(extent))]
    result = result.at[tuple(spot)].set(least)
    longest = extent.index(max(extent))
    spot[longest] = (spot[longest] + 1) % extent[longest]
    return result.at[tuple(spot)].set(largest)


def setup_inputs(seed: int = 0) -> dict:
    key_list = jax.random.split(jax.random.key(seed), 5)
    return {
        "positions": draw_positions(jax.random.fold_in(key_list[4], 71), 0),
        "pair_list": draw_pair_list(jax.random.fold_in(key_list[4], 71), 0),
        "pair_count": draw_pair_count(jax.random.fold_in(key_list[4], 71), 0),
        "active": set_ends((jax.random.randint(key_list[3], (LEAVES,), 0, 4) < 3).astype(jnp.int32), jax.random.fold_in(key_list[3], 1), 0, 1),
    }


def pair_kernel(first, second):
    dx = second[:3, None, :] - first[:3, :, None]
    r2 = lax.optimization_barrier(jnp.sum(dx * dx, axis=0)) + 0.09
    dist = jnp.sqrt(r2)
    kern = (lax.erfc(dist * 0.5) + dist * (1.0 / math.sqrt(math.pi)) * jnp.exp(-r2 * 0.25)) / (r2 * dist)
    weighted = dx * kern[None, :, :]
    on_first = lax.optimization_barrier(jnp.sum(weighted * second[3][None, None, :], axis=2))
    on_second = -lax.optimization_barrier(jnp.sum(weighted * first[3][None, :, None], axis=1))
    return (on_first, on_second)

def reference(positions, pair_list, pair_count, active):
    span = LEAF_DEV * N_LOCAL
    window = 5 * LEAF_DEV
    total = jnp.zeros((positions.shape[0], 3, positions.shape[2]), jnp.float32)
    rows = jnp.arange(pair_list.shape[0], dtype=jnp.int32)

    def step(acc, inputs):
        row, pair = inputs
        device = row // PAIR_DEV
        live = row % PAIR_DEV < pair_count[device]
        region_id = device // N_LOCAL
        place = device % N_LOCAL
        owner = device * LEAF_DEV + pair[0]
        index = pair[1]
        hop = index // window
        offset = index % window // LEAF_DEV - 2
        leaf = index % LEAF_DEV
        partner = (region_id + hop) % N_REGION * span + (place + offset) % N_LOCAL * LEAF_DEV + leaf

        def hit(acc):
            on_first, on_second = pair_kernel(positions[owner], positions[partner])
            acc = acc.at[owner].add(on_first)
            return acc.at[partner].add(on_second)
        return (lax.cond(live, hit, lambda value: value, acc), None)
    total, unused = lax.scan(step, total, (rows, pair_list))
    return total * active.astype(jnp.float32)[:, None, None]
```

```python
import math

import jax
import jax.numpy as jnp
from jax import lax
from jax.experimental import pallas as pl
from jax.experimental.pallas import tpu as pltpu
from jax.sharding import PartitionSpec as P

F32 = jnp.float32
BF16 = jnp.bfloat16
I32 = jnp.int32
MESH = pl.DeviceIdType.MESH

SHARDS = 10
SLOTS = 8
ROWS = 8
LANES = 128
OWN = 2

SHIFT = 4.75
ERFCX = (
    -0.0001473139400949286,
    1.1441739139316924,
    4.715090554694223,
    36.5304177576356,
    -63.44030619869776,
    1227.393340985424,
    -1993.351622536244,
)
INV_SQRT_PI = 1.0 / math.sqrt(math.pi)
EXP2_SCALE = -0.25 / math.log(2.0)


def thirds(value):
    high = value.astype(BF16)
    rest = value - high.astype(F32)
    middle = rest.astype(BF16)
    low = (rest - middle.astype(F32)).astype(BF16)
    return high, middle, low


def picked(choice, value):
    total = None
    for part in reversed(thirds(value)):
        term = jnp.dot(choice, part, preferred_element_type=F32)
        total = term if total is None else total + term
    return total


def place_of(shard):
    return shard // 5, shard % 5 - 2


def neighbours(shard, sign, n_region, n_local):
    hop, offset = place_of(shard)
    region = lax.rem(lax.axis_index("region") + sign * hop + n_region, n_region)
    local = lax.rem(lax.axis_index("local") + sign * offset + n_local, n_local)
    return (region, local)


def greet(sign, n_region, n_local):
    barrier = pltpu.get_barrier_semaphore()
    for shard in range(SHARDS):
        if shard != OWN:
            pl.semaphore_signal(
                barrier,
                inc=1,
                device_id=neighbours(shard, sign, n_region, n_local),
                device_id_type=MESH,
            )
    return barrier


def push_kernel(n_region, n_local, leaves, pairs, count, msg, meta, back, over, out_msg, out_meta,
                send_sem, recv_sem, send_meta_sem, recv_meta_sem, own_sem):
    barrier = greet(-1, n_region, n_local)
    n_leaf = leaves.shape[0] // ROWS
    n_pair = pairs.shape[1]
    owner = pairs[0:1, :]
    index = pairs[1:2, :]
    shard = lax.shift_right_logical(index, 6)
    leaf = lax.bitwise_and(index, 63)
    slot = lax.broadcasted_iota(I32, (1, n_pair), 1)
    live = slot < count[0:1, 0:1]
    member = (lax.broadcasted_iota(I32, (16, n_pair), 0) == shard) & live
    member = member.astype(F32)
    before = lax.broadcasted_iota(I32, (n_pair, n_pair), 0) < lax.broadcasted_iota(I32, (n_pair, n_pair), 1)
    ahead = jnp.dot(member.astype(BF16), before.astype(F32).astype(BF16), preferred_element_type=F32)
    rank = jnp.sum(member * ahead, axis=0, keepdims=True).astype(I32)
    fits = live & (rank < SLOTS)
    seat = jnp.where(fits, shard * SLOTS + rank, -1)
    over[...] = jnp.broadcast_to(
        jnp.max(jnp.where(live & (rank >= SLOTS), 1, 0), axis=1, keepdims=True), over.shape
    )
    total = SHARDS * SLOTS
    seated = (lax.broadcasted_iota(I32, (total, n_pair), 0) == seat).astype(F32).astype(BF16)
    owned = (lax.broadcasted_iota(I32, (n_leaf, n_pair), 0) == owner).astype(F32).astype(BF16)
    last = (((1,), (1,)), ((), ()))
    choice = lax.dot_general(seated, owned, last, preferred_element_type=F32).astype(BF16)
    back[...] = lax.dot_general(owned, seated, last, preferred_element_type=F32).astype(BF16)
    named = jnp.broadcast_to((leaf + 1).astype(F32), (LANES, n_pair)).astype(BF16)
    partner = lax.dot_general(seated, named, last, preferred_element_type=F32).astype(I32) - 1
    for h in range(SHARDS):
        out_meta[h] = partner[h * SLOTS : (h + 1) * SLOTS, :]
    for row in range(ROWS):
        plane = picked(choice, leaves[pl.ds(row, n_leaf, stride=ROWS), :])
        for h in range(SHARDS):
            out_msg[h, row * SLOTS : (row + 1) * SLOTS, :] = plane[h * SLOTS : (h + 1) * SLOTS, :]

    keep_msg = pltpu.make_async_copy(out_msg.at[OWN], msg.at[OWN], own_sem.at[0])
    keep_meta = pltpu.make_async_copy(out_meta.at[OWN], meta.at[OWN], own_sem.at[1])
    keep_msg.start()
    keep_meta.start()
    pl.semaphore_wait(barrier, SHARDS - 1)
    copies = []
    for h in range(SHARDS):
        if h == OWN:
            continue
        target = neighbours(h, 1, n_region, n_local)
        for source, dest, send, recv in (
            (out_meta, meta, send_meta_sem, recv_meta_sem),
            (out_msg, msg, send_sem, recv_sem),
        ):
            copy = pltpu.make_async_remote_copy(
                src_ref=source.at[h],
                dst_ref=dest.at[h],
                send_sem=send.at[h],
                recv_sem=recv.at[h],
                device_id=target,
                device_id_type=MESH,
            )
            copy.start()
            copies.append(copy)
    for copy in copies:
        copy.wait()
    keep_msg.wait()
    keep_meta.wait()


def push(leaves, pairs, count, n_region, n_local):
    vmem = pl.BlockSpec(memory_space=pltpu.VMEM)
    anywhere = pl.BlockSpec(memory_space=pl.ANY)
    n_leaf = leaves.shape[0] // ROWS

    def kernel(*refs):
        push_kernel(n_region, n_local, *refs)

    return pl.pallas_call(
        kernel,
        out_shape=(
            jax.ShapeDtypeStruct((SHARDS, ROWS * SLOTS, LANES), F32),
            jax.ShapeDtypeStruct((SHARDS, SLOTS, LANES), I32),
            jax.ShapeDtypeStruct((n_leaf, SHARDS * SLOTS), BF16),
            jax.ShapeDtypeStruct((8, LANES), I32),
        ),
        in_specs=[vmem, vmem, vmem],
        out_specs=(anywhere, anywhere, vmem, vmem),
        scratch_shapes=[
            pltpu.VMEM((SHARDS, ROWS * SLOTS, LANES), F32),
            pltpu.VMEM((SHARDS, SLOTS, LANES), I32),
            pltpu.SemaphoreType.DMA((SHARDS,)),
            pltpu.SemaphoreType.DMA((SHARDS,)),
            pltpu.SemaphoreType.DMA((SHARDS,)),
            pltpu.SemaphoreType.DMA((SHARDS,)),
            pltpu.SemaphoreType.DMA((2,)),
        ],
        compiler_params=pltpu.CompilerParams(
            collective_id=0, has_side_effects=True, vmem_limit_bytes=32 * 2**20
        ),
        name="push",
    )(leaves, pairs, count)


def pair_strength(first, second):
    dx = second[0] - first[0]
    dy = second[1] - first[1]
    dz = second[2] - first[2]
    r2 = dx * dx + dy * dy + (dz * dz + 0.09)
    inverse = lax.rsqrt(r2)
    near = pl.reciprocal(r2 * inverse + SHIFT, approx=True)
    series = near * ERFCX[-1] + ERFCX[-2]
    for coefficient in ERFCX[-3::-1]:
        series = series * near + coefficient
    decay = jnp.exp2(r2 * EXP2_SCALE)
    return (series * inverse + INV_SQRT_PI) * ((inverse * inverse) * decay)


def weights(tile, centre):
    row = lax.broadcasted_iota(I32, (ROWS, LANES), 0)
    low = row < 4
    mass = jnp.where(
        low, jnp.broadcast_to(tile[3:4], (ROWS, LANES)), jnp.broadcast_to(tile[7:8], (ROWS, LANES))
    )
    shifted = tile - centre
    weighted = jnp.where(row % 4 == 3, mass, shifted * mass)
    a, b, c = (part.astype(F32) for part in thirds(weighted))
    a_up, b_up, c_up = (pltpu.roll(part, 4, 0) for part in (a, b, c))
    none = jnp.zeros_like(c)
    top = jnp.concatenate([jnp.where(low, a, b_up), jnp.where(low, a_up, b)], axis=1)
    bottom = jnp.concatenate([jnp.where(low, c, none), jnp.where(low, c_up, none)], axis=1)
    return shifted, jnp.concatenate([top, bottom], axis=0).astype(BF16)


def force(sums, shifted):
    top, bottom = sums[:8], sums[8:]
    joined = top + pltpu.roll(top, 4, 0) + bottom
    low = lax.broadcasted_iota(I32, (ROWS, LANES), 0) < 4
    tile = jnp.where(low, joined[:, :LANES], pltpu.roll(joined[:, LANES:], 4, 0))
    pull = jnp.where(
        low, jnp.broadcast_to(tile[3:4], (ROWS, LANES)), jnp.broadcast_to(tile[7:8], (ROWS, LANES))
    )
    return tile - shifted * pull


def pair_kernel(meta, own, msg, on_partner, on_owner, live, high, low_part, w_owner, w_partner, s_owner, s_partner):
    for ref in (on_partner, on_owner, high, low_part, w_owner, w_partner, s_owner, s_partner):
        ref[...] = jnp.zeros_like(ref)
    block = 16

    def note(slot, n):
        live[n] = slot
        return n + jnp.where(meta[slot, 0] >= 0, 1, 0)

    n_live = lax.fori_loop(0, SHARDS * SLOTS, note, jnp.int32(0))
    live[n_live] = 0

    def slot_rows(slot):
        return pl.ds(slot // SLOTS * (ROWS * SLOTS) + slot % SLOTS, ROWS, stride=SLOTS)

    def step(turn, before):
        now = live[turn]
        leaf = jnp.maximum(meta[now, 0], 0)
        here = turn % 2
        there = 1 - here
        plain = (((1,), (0,)), ((), ()))
        turned = (((1,), (1,)), ((), ()))
        wo, wp, kh, kl = w_owner[there], w_partner[there], high[there], low_part[there]
        to_partner = lax.dot_general(wo, kh, plain, preferred_element_type=F32) + lax.dot_general(
            wo, kl, plain, preferred_element_type=F32
        )
        to_owner = lax.dot_general(wp, kh, turned, preferred_element_type=F32) + lax.dot_general(
            wp, kl, turned, preferred_element_type=F32
        )
        leaf_before = jnp.maximum(meta[before, 0], 0)
        on_partner[leaf_before] = on_partner[leaf_before] + force(to_partner, s_partner[there])
        on_owner[slot_rows(before), :] = force(to_owner, s_owner[there])

        first = msg[slot_rows(now), :]
        second = own[leaf]
        low = lax.broadcasted_iota(I32, (ROWS, LANES), 0) < 4
        centre = jnp.broadcast_to(first[:, 0:1], (ROWS, LANES))
        centre = jnp.where(low, centre, pltpu.roll(centre, 4, 0))
        s_owner[here], w_owner[here] = weights(first, centre)
        s_partner[here], w_partner[here] = weights(second, centre)
        column = jnp.transpose(first)
        for half in range(2):
            for top in range(0, LANES, block):
                xi = [
                    jnp.broadcast_to(column[top : top + block, half * 4 + c : half * 4 + c + 1], (block, LANES))
                    for c in range(3)
                ]
                for side in range(2):
                    xj = [
                        jnp.broadcast_to(second[side * 4 + c : side * 4 + c + 1], (block, LANES)) for c in range(3)
                    ]
                    strength = pair_strength(xi, xj)
                    part = strength.astype(BF16)
                    rest = (strength - part.astype(F32)).astype(BF16)
                    rows = slice(half * LANES + top, half * LANES + top + block)
                    lanes = slice(side * LANES, (side + 1) * LANES)
                    high[here, rows, lanes] = part
                    low_part[here, rows, lanes] = rest
        return now

    lax.fori_loop(0, n_live + 1, step, jnp.int32(0))


def pair_forces(meta, own, msg):
    vmem = pl.BlockSpec(memory_space=pltpu.VMEM)
    width = 2 * LANES
    return pl.pallas_call(
        pair_kernel,
        out_shape=(
            jax.ShapeDtypeStruct(own.shape, F32),
            jax.ShapeDtypeStruct(msg.shape, F32),
        ),
        in_specs=[pl.BlockSpec(memory_space=pltpu.SMEM), vmem, vmem],
        out_specs=(vmem, vmem),
        scratch_shapes=[
            pltpu.SMEM((SHARDS * SLOTS + 1,), I32),
            pltpu.VMEM((2, width, width), BF16),
            pltpu.VMEM((2, width, width), BF16),
            pltpu.VMEM((2, 16, width), BF16),
            pltpu.VMEM((2, 16, width), BF16),
            pltpu.VMEM((2, ROWS, LANES), F32),
            pltpu.VMEM((2, ROWS, LANES), F32),
        ],
        compiler_params=pltpu.CompilerParams(vmem_limit_bytes=32 * 2**20),
        name="pair_forces",
    )(meta, own, msg)


def give_back_kernel(n_region, n_local, on_owner, on_partner, back, total, landed, send_sem, recv_sem, own_sem):
    barrier = greet(1, n_region, n_local)
    keep = pltpu.make_async_copy(on_owner.at[OWN], landed.at[OWN], own_sem)
    keep.start()
    pl.semaphore_wait(barrier, SHARDS - 1)
    copies = []
    for h in range(SHARDS):
        if h == OWN:
            continue
        copy = pltpu.make_async_remote_copy(
            src_ref=on_owner.at[h],
            dst_ref=landed.at[h],
            send_sem=send_sem.at[h],
            recv_sem=recv_sem.at[h],
            device_id=neighbours(h, -1, n_region, n_local),
            device_id_type=MESH,
        )
        copy.start()
        copies.append(copy)
    keep.wait()
    for copy in copies:
        copy.wait()
    choice = back[...]
    n_leaf = total.shape[1]
    for half in range(2):
        for c in range(3):
            row = half * 4 + c
            forces = jnp.concatenate(
                [landed[h, row * SLOTS : (row + 1) * SLOTS, :] for h in range(SHARDS)], axis=0
            )
            total[c, :, half * LANES : (half + 1) * LANES] = (
                picked(choice, forces) + on_partner[pl.ds(row, n_leaf, stride=ROWS), :]
            )


def give_back(on_owner, on_partner, back, n_region, n_local):
    vmem = pl.BlockSpec(memory_space=pltpu.VMEM)
    n_leaf = on_partner.shape[0] // ROWS

    def kernel(*refs):
        give_back_kernel(n_region, n_local, *refs)

    return pl.pallas_call(
        kernel,
        out_shape=jax.ShapeDtypeStruct((3, n_leaf, 2 * LANES), F32),
        in_specs=[vmem, vmem, vmem],
        out_specs=vmem,
        scratch_shapes=[
            pltpu.VMEM((SHARDS, ROWS * SLOTS, LANES), F32),
            pltpu.SemaphoreType.DMA((SHARDS,)),
            pltpu.SemaphoreType.DMA((SHARDS,)),
            pltpu.SemaphoreType.DMA,
        ],
        compiler_params=pltpu.CompilerParams(
            collective_id=1, has_side_effects=True, vmem_limit_bytes=32 * 2**20
        ),
        name="give_back",
    )(on_owner, on_partner, back)


def passed_along(value, axis, steps):
    if steps == 0:
        return value
    count = lax.axis_size(axis)
    pairs = [(source, (source + steps) % count) for source in range(count)]
    return lax.ppermute(value, axis, pairs)


def dense_pair(first, second):
    dx = second[:3, None, :] - first[:3, :, None]
    r2 = jnp.sum(dx * dx, axis=0) + 0.09
    dist = jnp.sqrt(r2)
    kern = (lax.erfc(dist * 0.5) + dist * INV_SQRT_PI * jnp.exp(-r2 * 0.25)) / (r2 * dist)
    weighted = dx * kern[None, :, :]
    on_first = jnp.sum(weighted * second[3][None, None, :], axis=2)
    on_second = -jnp.sum(weighted * first[3][None, :, None], axis=1)
    return (on_first, on_second)


def by_windows(positions, pair_list, pair_count):
    leaf_dev, _, width = positions.shape
    offsets = (-2, -1, 0, 1, 2)
    here = jnp.concatenate([passed_along(positions, "local", -offset) for offset in offsets], axis=0)
    table = jnp.concatenate([here, passed_along(here, "region", -1)], axis=0)
    span = here.shape[0]
    slots = pair_list.shape[0]
    alive = (jnp.arange(slots, dtype=I32) < pair_count[0]).astype(F32)

    def step(carry, inputs):
        own_part, react_part = carry
        pair, weight = inputs
        on_first, on_second = dense_pair(positions[pair[0]], table[pair[1]])
        own_part = own_part.at[pair[0]].add(on_first * weight)
        react_part = react_part.at[pair[1]].add(on_second * weight)
        return ((own_part, react_part), None)

    own_part = jnp.zeros((leaf_dev, 3, width), F32)
    reaction = jnp.zeros((2 * span, 3, width), F32)
    (own_part, reaction), _ = lax.scan(step, (own_part, reaction), (pair_list, alive))
    reaction = reaction[:span] + passed_along(reaction[span:], "region", 1)
    for place, offset in enumerate(offsets):
        piece = reaction[place * leaf_dev : (place + 1) * leaf_dev]
        own_part = own_part + passed_along(piece, "local", offset)
    return own_part.transpose(1, 0, 2)


def shards(positions, pair_list, pair_count, active):
    n_region = lax.axis_size("region")
    n_local = lax.axis_size("local")
    n_leaf, n_row, width = positions.shape
    leaves = positions.reshape(n_leaf, n_row, 2, LANES).transpose(0, 2, 1, 3).reshape(n_leaf * ROWS, LANES)
    msg, meta, back, over = push(leaves, pair_list.T, pair_count.reshape(1, 1), n_region, n_local)
    crowded = lax.pmax(over[0, 0], ("region", "local"))
    on_partner, on_owner = pair_forces(
        meta.reshape(SHARDS * SLOTS, LANES),
        leaves.reshape(n_leaf, ROWS, LANES),
        msg.reshape(SHARDS * ROWS * SLOTS, LANES),
    )
    total = give_back(
        on_owner.reshape(SHARDS, ROWS * SLOTS, LANES),
        on_partner.reshape(n_leaf * ROWS, LANES),
        back,
        n_region,
        n_local,
    )
    total = lax.cond(
        crowded > 0,
        lambda total: by_windows(positions, pair_list, pair_count),
        lambda total: total,
        total,
    )
    return (total * active.astype(F32)[None, :, None]).transpose(1, 0, 2)


def solution(mesh):
    return jax.shard_map(
        shards,
        mesh=mesh,
        in_specs=(
            P(("region", "local"), None, None),
            P(("region", "local"), None),
            P(("region", "local")),
            P(("region", "local")),
        ),
        out_specs=P(("region", "local"), None, None),
        check_vma=False,
    )
```

```python
import math

import jax
import jax.numpy as jnp
from jax import lax
from jax.experimental import pallas as pl
from jax.experimental.pallas import tpu as pltpu
from jax.sharding import PartitionSpec as P

F32 = jnp.float32
BF16 = jnp.bfloat16
I32 = jnp.int32
MESH = pl.DeviceIdType.MESH

SHARDS = 10
SEATS = 8
SLOTS = 7
ROWS = 8
LANES = 128
WIDTH = 2 * LANES
OWN = 2
BLOCK = 128

SHIFT = 0.25
ERFCX = (
    0.9999664993365988,
    -0.5639379807585301,
    0.10826155296772119,
    -0.0033908818915562877,
    -0.001816315565602909,
    0.00020140930421213982,
)
INV_SQRT_PI = 1.0 / math.sqrt(math.pi)
EXP2_SCALE = -0.25 / math.log(2.0)


def thirds(value):
    high = value.astype(BF16)
    rest = value - high.astype(F32)
    middle = rest.astype(BF16)
    low = (rest - middle.astype(F32)).astype(BF16)
    return high, middle, low


def picked(choice, value):
    total = None
    for part in reversed(thirds(value)):
        term = jnp.dot(choice, part, preferred_element_type=F32)
        total = term if total is None else total + term
    return total


def pair_strength(first, second):
    dx = second[0] - first[0]
    dy = second[1] - first[1]
    dz = second[2] - first[2]
    r2 = dx * dx + dy * dy + (dz * dz + 0.09)
    inverse = lax.rsqrt(r2)
    near = pl.reciprocal(inverse + SHIFT, approx=True)
    series = near * ERFCX[-1] + ERFCX[-2]
    for coefficient in ERFCX[-3::-1]:
        series = series * near + coefficient
    decay = jnp.exp2(r2 * EXP2_SCALE)
    return (series * inverse + INV_SQRT_PI) * ((inverse * inverse) * decay)


def in_halves(low_half, high_half):
    low = lax.broadcasted_iota(I32, (ROWS, LANES), 0) < 4
    return jnp.where(low, low_half, high_half)


def spread_rows(tile, row):
    return in_halves(
        jnp.broadcast_to(tile[row : row + 1], (ROWS, LANES)),
        jnp.broadcast_to(tile[row + 4 : row + 5], (ROWS, LANES)),
    )


def weights(tile, centre):
    row = lax.broadcasted_iota(I32, (ROWS, LANES), 0)
    shifted = tile - centre
    mass = spread_rows(tile, 3)
    weighted = jnp.where(row % 4 == 3, mass, shifted * mass)
    a, b, c = (part.astype(F32) for part in thirds(weighted))
    a_up, b_up, c_up = (pltpu.roll(part, 4, 0) for part in (a, b, c))
    none = jnp.zeros_like(c)
    top = jnp.concatenate([in_halves(a, b_up), in_halves(a_up, b)], axis=1)
    bottom = jnp.concatenate([in_halves(c, none), in_halves(c_up, none)], axis=1)
    return shifted, jnp.concatenate([top, bottom], axis=0).astype(BF16)


def force(sums, shifted):
    top, bottom = sums[:8], sums[8:]
    joined = top + pltpu.roll(top, 4, 0) + bottom
    tile = in_halves(joined[:, :LANES], pltpu.roll(joined[:, LANES:], 4, 0))
    return tile - shifted * spread_rows(tile, 3)


def spreader(half):
    row = lax.broadcasted_iota(I32, (32, 3 * LANES), 0)
    lane = lax.broadcasted_iota(I32, (32, 3 * LANES), 1)
    chosen = (row < 24) & (row % 8 == half * 4 + lane // LANES)
    return chosen.astype(F32).astype(BF16)


class Stage:
    shapes = (
        ((WIDTH, 3 * LANES), F32),
        ((ROWS, LANES), F32),
        ((16, WIDTH), BF16),
        ((16, WIDTH), BF16),
        ((ROWS, LANES), F32),
        ((ROWS, LANES), F32),
        ((WIDTH, WIDTH), BF16),
        ((WIDTH, WIDTH), BF16),
    )

    def __init__(self, refs):
        (self.columns, self.second, self.w_owner, self.w_partner,
         self.s_owner, self.s_partner, self.high, self.low) = refs

    def clear(self):
        for ref in (self.w_owner, self.w_partner, self.s_owner, self.s_partner, self.high, self.low):
            ref[...] = jnp.zeros_like(ref)

    def prepare(self, first, second, spread):
        corner = jnp.broadcast_to(first[:, 0:1], (ROWS, LANES))
        centre = in_halves(corner, pltpu.roll(corner, 4, 0))
        self.s_owner[...], self.w_owner[...] = weights(first, centre)
        self.s_partner[...], self.w_partner[...] = weights(second, centre)
        self.second[...] = second
        a, b, c = (part.astype(F32) for part in thirds(first))
        parts = jnp.transpose(jnp.concatenate([a, b, c, jnp.zeros_like(a)], axis=0)).astype(BF16)
        for half in range(2):
            self.columns[half * LANES : (half + 1) * LANES, :] = jnp.dot(
                parts, spread[half], preferred_element_type=F32
            )

    def strengths(self):
        second = self.second[...]
        for top in range(0, WIDTH, BLOCK):
            rows = slice(top, top + BLOCK)
            xi = [self.columns[rows, c * LANES : (c + 1) * LANES] for c in range(3)]
            for side in range(2):
                xj = [jnp.broadcast_to(second[side * 4 + c : side * 4 + c + 1], (BLOCK, LANES)) for c in range(3)]
                strength = pair_strength(xi, xj)
                part = strength.astype(BF16)
                lanes = slice(side * LANES, (side + 1) * LANES)
                self.high[rows, lanes] = part
                self.low[rows, lanes] = (strength - part.astype(F32)).astype(BF16)

    def sums(self):
        plain = (((1,), (0,)), ((), ()))
        turned = (((1,), (1,)), ((), ()))
        wo, wp, high, low = self.w_owner[...], self.w_partner[...], self.high[...], self.low[...]
        to_partner = lax.dot_general(wo, high, plain, preferred_element_type=F32) + lax.dot_general(
            wo, low, plain, preferred_element_type=F32
        )
        to_owner = lax.dot_general(wp, high, turned, preferred_element_type=F32) + lax.dot_general(
            wp, low, turned, preferred_element_type=F32
        )
        return force(to_partner, self.s_partner[...]), force(to_owner, self.s_owner[...])


def forces_kernel(n_region, n_local, leaves, pairs, count, total, over,
                  out_msg, out_meta, msg, meta, partners, named, on_partner, on_owner, landed,
                  flag_out, flag_in, spread,
                  msg_send, msg_recv, meta_send, meta_recv, back_send, back_recv, flag_send, flag_recv,
                  *stage_refs):
    here_region = lax.axis_index("region")
    here_local = lax.axis_index("local")
    n_leaf = leaves.shape[0] // ROWS
    n_pair = pairs.shape[1]
    n_seat = SHARDS * SEATS
    rounds = (n_region * n_local - 1).bit_length()
    per = len(Stage.shapes)
    stages = [Stage(stage_refs[i * per : (i + 1) * per]) for i in range(3)]
    last = (((1,), (1,)), ((), ()))

    def device(hop, offset):
        return (
            lax.rem(here_region + hop + n_region, n_region),
            lax.rem(here_local + offset + n_local, n_local),
        )

    def partner_device(h):
        return device(h // 5, h % 5 - 2)

    def lister_device(h):
        return device(-(h // 5), 2 - h % 5)

    barrier = pltpu.get_barrier_semaphore()
    friends = []
    for h in range(SHARDS):
        if h != OWN:
            friends += [(h // 5, h % 5 - 2), (-(h // 5), 2 - h % 5)]
    for step in range(rounds):
        stride = 2**step
        friend = (-(stride // n_local), -(stride % n_local))
        if friend not in friends:
            friends.append(friend)
    for friend in friends:
        pl.semaphore_signal(barrier, inc=1, device_id=device(*friend), device_id_type=MESH)

    owner = pairs[0:1, :]
    index = pairs[1:2, :]
    shard = index // 64
    leaf = index % 64
    live = lax.broadcasted_iota(I32, (1, n_pair), 1) < count[0:1, 0:1]
    member = ((lax.broadcasted_iota(I32, (16, n_pair), 0) == shard) & live).astype(F32)
    before = lax.broadcasted_iota(I32, (n_pair, n_pair), 0) < lax.broadcasted_iota(I32, (n_pair, n_pair), 1)
    ahead = jnp.dot(member.astype(BF16), before.astype(F32).astype(BF16), preferred_element_type=F32)
    rank = jnp.sum(member * ahead, axis=0, keepdims=True).astype(I32)
    seat = jnp.where(live & (rank < SLOTS), shard * SEATS + rank, -1)
    flag_out[0] = jnp.broadcast_to(
        jnp.max(jnp.where(live & (rank >= SLOTS), 1, 0), axis=1, keepdims=True), (8, LANES)
    )
    seated = (lax.broadcasted_iota(I32, (n_seat, n_pair), 0) == seat).astype(F32).astype(BF16)
    owned = (lax.broadcasted_iota(I32, (n_leaf, n_pair), 0) == owner).astype(F32).astype(BF16)
    choice = lax.dot_general(seated, owned, last, preferred_element_type=F32).astype(BF16)
    back = lax.dot_general(owned, seated, last, preferred_element_type=F32).astype(BF16)
    names = jnp.broadcast_to((leaf + 1).astype(F32), (LANES, n_pair)).astype(BF16)
    partner = lax.dot_general(seated, names, last, preferred_element_type=F32).astype(I32) - 1
    for h in range(SHARDS):
        out_meta[h] = partner[h * SEATS : (h + 1) * SEATS, :]
    for row in range(ROWS):
        plane = picked(choice, leaves[pl.ds(row, n_leaf, stride=ROWS), :])
        for h in range(SHARDS):
            out_msg[h, row * SEATS : (row + 1) * SEATS, :] = plane[h * SEATS : (h + 1) * SEATS, :]

    def message(h):
        return pltpu.make_async_remote_copy(
            src_ref=out_msg.at[h], dst_ref=msg.at[h], send_sem=msg_send.at[h], recv_sem=msg_recv.at[h],
            device_id=partner_device(h), device_id_type=MESH,
        )

    def names_of(h):
        return pltpu.make_async_remote_copy(
            src_ref=out_meta.at[h], dst_ref=meta.at[h], send_sem=meta_send.at[h], recv_sem=meta_recv.at[h],
            device_id=partner_device(h), device_id_type=MESH,
        )

    def answer(h):
        return pltpu.make_async_remote_copy(
            src_ref=on_owner.at[h], dst_ref=landed.at[h], send_sem=back_send.at[h], recv_sem=back_recv.at[h],
            device_id=lister_device(h), device_id_type=MESH,
        )

    def flag(step, stride):
        return pltpu.make_async_remote_copy(
            src_ref=flag_out.at[step], dst_ref=flag_in.at[step],
            send_sem=flag_send.at[step], recv_sem=flag_recv.at[step],
            device_id=device(stride // n_local, stride % n_local), device_id_type=MESH,
        )

    pl.semaphore_wait(barrier, len(friends))
    others = [(OWN + place) % SHARDS for place in range(1, SHARDS)]
    for h in others:
        names_of(h).start()
    for h in others:
        message(h).start()
    flag(0, 1).start()

    for half in range(2):
        spread[half] = spreader(half)
    for stage in stages:
        stage.clear()
    on_partner[...] = jnp.zeros_like(on_partner)
    on_owner[...] = jnp.zeros_like(on_owner)
    msg[OWN] = out_msg[OWN]
    meta[OWN] = out_meta[OWN]

    def gather(shards_here):
        rows = len(shards_here) * SEATS
        seats = jnp.concatenate([meta[h] for h in shards_here], axis=0)
        wanted = (seats == lax.broadcasted_iota(I32, (rows, LANES), 1)).astype(F32).astype(BF16)
        for place, h in enumerate(shards_here):
            named[h] = wanted[place * SEATS : (place + 1) * SEATS].astype(F32)
        for row in range(ROWS):
            plane = picked(wanted[:, :n_leaf], leaves[pl.ds(row, n_leaf, stride=ROWS), :])
            for place, h in enumerate(shards_here):
                partners[h, row * SEATS : (row + 1) * SEATS, :] = plane[place * SEATS : (place + 1) * SEATS, :]

    def prepare(stage, h, slot):
        seat_rows = pl.ds(slot, ROWS, stride=SEATS)
        stage.prepare(msg[h, seat_rows, :], partners[h, seat_rows, :], spread)

    def finish(stage, h, slot):
        seat_rows = pl.ds(slot, ROWS, stride=SEATS)
        on_partner[h, seat_rows, :], on_owner[h, seat_rows, :] = stage.sums()

    def stage_of(slot):
        return stages[2 if slot == SLOTS - 1 else slot % 2]

    gather([OWN])
    prepare(stage_of(0), OWN, 0)

    def turn(place, stride):
        h = lax.rem(OWN + place, SHARDS)
        h_before = lax.rem(OWN + place + SHARDS - 1, SHARDS)
        h_next = lax.rem(OWN + place + 1, SHARDS)
        finish(stage_of(SLOTS - 1), h_before, SLOTS - 1)
        stage_of(0).strengths()
        prepare(stage_of(1), h, 1)

        @pl.when(place >= 2)
        def _():
            answer(h_before).start()

        @pl.when(place == 0)
        def _():
            for other in others:
                names_of(other).wait_recv()
            gather(others)

        @pl.when(place < SHARDS - 1)
        def _():
            message(h_next).wait_recv()

        @pl.when(place < rounds)
        def _():
            flag(place, stride).wait()
            flag_out[place + 1] = jnp.maximum(flag_out[place], flag_in[place])

        @pl.when(place < rounds - 1)
        def _():
            flag(place + 1, stride * 2).start()

        for slot in range(1, SLOTS):
            finish(stage_of(slot - 1), h, slot - 1)
            stage_of(slot).strengths()
            if slot + 1 < SLOTS:
                prepare(stage_of(slot + 1), h, slot + 1)
        prepare(stage_of(0), h_next, 0)
        return stride * 2

    lax.fori_loop(0, SHARDS, turn, jnp.int32(1))
    h_end = others[-1]
    finish(stage_of(SLOTS - 1), h_end, SLOTS - 1)
    answer(h_end).start()
    over[...] = flag_out[rounds]
    for h in others:
        names_of(h).wait_send()
        message(h).wait_send()
    for h in others:
        answer(h).wait()

    wanted = jnp.concatenate([named[h] for h in range(SHARDS)], axis=0).astype(BF16)
    first = (((0,), (0,)), ((), ()))
    for half in range(2):
        for c in range(3):
            rows = slice((half * 4 + c) * SEATS, (half * 4 + c + 1) * SEATS)
            listed = jnp.concatenate(
                [(on_owner if h == OWN else landed)[h, rows, :] for h in range(SHARDS)], axis=0
            )
            met = jnp.concatenate([on_partner[h, rows, :] for h in range(SHARDS)], axis=0)
            result = None
            for part, other in zip(thirds(listed)[::-1], thirds(met)[::-1]):
                term = jnp.dot(back, part, preferred_element_type=F32) + lax.dot_general(
                    wanted, other, first, preferred_element_type=F32
                )[:n_leaf]
                result = term if result is None else result + term
            total[c, :, half * LANES : (half + 1) * LANES] = result


def forces(leaves, pairs, count, n_region, n_local):
    vmem = pl.BlockSpec(memory_space=pltpu.VMEM)
    n_leaf = leaves.shape[0] // ROWS
    rounds = (n_region * n_local - 1).bit_length()
    message = pltpu.VMEM((SHARDS, ROWS * SEATS, LANES), F32)
    names = pltpu.VMEM((SHARDS, SEATS, LANES), I32)

    def kernel(*refs):
        forces_kernel(n_region, n_local, *refs)

    return pl.pallas_call(
        kernel,
        out_shape=(
            jax.ShapeDtypeStruct((3, n_leaf, WIDTH), F32),
            jax.ShapeDtypeStruct((8, LANES), I32),
        ),
        in_specs=[vmem, vmem, vmem],
        out_specs=(vmem, vmem),
        scratch_shapes=[
            message,
            names,
            message,
            names,
            message,
            pltpu.VMEM((SHARDS, SEATS, LANES), F32),
            message,
            message,
            message,
            pltpu.VMEM((rounds + 1, 8, LANES), I32),
            pltpu.VMEM((rounds + 1, 8, LANES), I32),
            pltpu.VMEM((2, 32, 3 * LANES), BF16),
        ]
        + [pltpu.SemaphoreType.DMA((SHARDS,))] * 6
        + [pltpu.SemaphoreType.DMA((rounds,))] * 2
        + [pltpu.VMEM(*shape) for shape in Stage.shapes] * 3,
        compiler_params=pltpu.CompilerParams(
            collective_id=0, has_side_effects=True, vmem_limit_bytes=32 * 2**20
        ),
        name="forces",
    )(leaves, pairs, count)


def passed_along(value, axis, steps):
    if steps == 0:
        return value
    count = lax.axis_size(axis)
    pairs = [(source, (source + steps) % count) for source in range(count)]
    return lax.ppermute(value, axis, pairs)


def dense_pair(first, second):
    dx = second[:3, None, :] - first[:3, :, None]
    r2 = jnp.sum(dx * dx, axis=0) + 0.09
    dist = jnp.sqrt(r2)
    kern = (lax.erfc(dist * 0.5) + dist * INV_SQRT_PI * jnp.exp(-r2 * 0.25)) / (r2 * dist)
    weighted = dx * kern[None, :, :]
    on_first = jnp.sum(weighted * second[3][None, None, :], axis=2)
    on_second = -jnp.sum(weighted * first[3][None, :, None], axis=1)
    return (on_first, on_second)


def by_windows(positions, pair_list, pair_count):
    leaf_dev, _, width = positions.shape
    offsets = (-2, -1, 0, 1, 2)
    here = jnp.concatenate([passed_along(positions, "local", -offset) for offset in offsets], axis=0)
    table = jnp.concatenate([here, passed_along(here, "region", -1)], axis=0)
    span = here.shape[0]
    slots = pair_list.shape[0]
    alive = (jnp.arange(slots, dtype=I32) < pair_count[0]).astype(F32)

    def step(carry, inputs):
        own_part, react_part = carry
        pair, weight = inputs
        on_first, on_second = dense_pair(positions[pair[0]], table[pair[1]])
        own_part = own_part.at[pair[0]].add(on_first * weight)
        react_part = react_part.at[pair[1]].add(on_second * weight)
        return ((own_part, react_part), None)

    own_part = jnp.zeros((leaf_dev, 3, width), F32)
    reaction = jnp.zeros((2 * span, 3, width), F32)
    (own_part, reaction), _ = lax.scan(step, (own_part, reaction), (pair_list, alive))
    reaction = reaction[:span] + passed_along(reaction[span:], "region", 1)
    for place, offset in enumerate(offsets):
        piece = reaction[place * leaf_dev : (place + 1) * leaf_dev]
        own_part = own_part + passed_along(piece, "local", offset)
    return own_part.transpose(1, 0, 2)


def shards(positions, pair_list, pair_count, active):
    n_region = lax.axis_size("region")
    n_local = lax.axis_size("local")
    n_leaf, n_row, width = positions.shape
    leaves = positions.reshape(n_leaf, n_row, 2, LANES).transpose(0, 2, 1, 3).reshape(n_leaf * ROWS, LANES)
    total, over = forces(leaves, pair_list.T, pair_count.reshape(1, 1), n_region, n_local)
    total = lax.cond(
        over[0, 0] > 0,
        lambda total: by_windows(positions, pair_list, pair_count),
        lambda total: total,
        total,
    )
    return (total * active.astype(F32)[None, :, None]).transpose(1, 0, 2)


def solution(mesh):
    return jax.shard_map(
        shards,
        mesh=mesh,
        in_specs=(
            P(("region", "local"), None, None),
            P(("region", "local"), None),
            P(("region", "local")),
            P(("region", "local")),
        ),
        out_specs=P(("region", "local"), None, None),
        check_vma=False,
    )
```

```python
import math

import jax
import jax.numpy as jnp
from jax import lax
from jax.experimental import pallas as pl
from jax.experimental.pallas import tpu as pltpu
from jax.sharding import PartitionSpec as P

F32 = jnp.float32
BF16 = jnp.bfloat16
I32 = jnp.int32
MESH = pl.DeviceIdType.MESH

SHARDS = 10
SEATS = 8
SLOTS = 7
ROWS = 8
LANES = 128
WIDTH = 2 * LANES
OWN = 2
BLOCK = 32

SHIFT = 0.25
ERFCX = (
    0.9999664993365988,
    -0.5639379807585301,
    0.10826155296772119,
    -0.0033908818915562877,
    -0.001816315565602909,
    0.00020140930421213982,
)
INV_SQRT_PI = 1.0 / math.sqrt(math.pi)

UNIT = math.sqrt(0.25 / math.log(2.0))
SOFTENING = 0.09 * UNIT**2
UNIT_SHIFT = SHIFT / UNIT
UNIT_ERFCX = tuple(c * UNIT ** (2 - n) for n, c in enumerate(ERFCX))
UNIT_TAIL = UNIT * INV_SQRT_PI


def thirds(value):
    high = value.astype(BF16)
    rest = value - high.astype(F32)
    middle = rest.astype(BF16)
    low = (rest - middle.astype(F32)).astype(BF16)
    return high, middle, low


def picked(choice, value):
    total = None
    for part in reversed(thirds(value)):
        term = jnp.dot(choice, part, preferred_element_type=F32)
        total = term if total is None else total + term
    return total


def pair_strength(first, second):
    dx = second[0] - first[0]
    dy = second[1] - first[1]
    dz = second[2] - first[2]
    r2 = dx * dx + dy * dy + (dz * dz + SOFTENING)
    inverse = lax.rsqrt(r2)
    near = pl.reciprocal(inverse + UNIT_SHIFT, approx=True)
    series = near * UNIT_ERFCX[-1] + UNIT_ERFCX[-2]
    for coefficient in UNIT_ERFCX[-3::-1]:
        series = series * near + coefficient
    return (series * inverse + UNIT_TAIL) * pl.reciprocal(r2 * jnp.exp2(r2), approx=True)


def in_halves(low_half, high_half):
    low = lax.broadcasted_iota(I32, (ROWS, LANES), 0) < 4
    return jnp.where(low, low_half, high_half)


def spread_rows(tile, row):
    return in_halves(
        jnp.broadcast_to(tile[row : row + 1], (ROWS, LANES)),
        jnp.broadcast_to(tile[row + 4 : row + 5], (ROWS, LANES)),
    )


def weights(tile, centre):
    row = lax.broadcasted_iota(I32, (ROWS, LANES), 0)
    shifted = (tile - centre) * UNIT
    mass = spread_rows(tile, 3)
    weighted = jnp.where(row % 4 == 3, mass, shifted * mass)
    a, b, c = (part.astype(F32) for part in thirds(weighted))
    a_up, b_up, c_up = (pltpu.roll(part, 4, 0) for part in (a, b, c))
    none = jnp.zeros_like(c)
    top = jnp.concatenate([in_halves(a, b_up), in_halves(a_up, b)], axis=1)
    bottom = jnp.concatenate([in_halves(c, none), in_halves(c_up, none)], axis=1)
    return shifted, jnp.concatenate([top, bottom], axis=0).astype(BF16)


def force(sums, shifted):
    top, bottom = sums[:8], sums[8:]
    joined = top + pltpu.roll(top, 4, 0) + bottom
    tile = in_halves(joined[:, :LANES], pltpu.roll(joined[:, LANES:], 4, 0))
    return tile - shifted * spread_rows(tile, 3)


def flag_rounds(n_device):
    rounds = []
    reach = 1
    while reach < n_device:
        radix = min(4, n_device // reach)
        rounds.append([reach * step for step in range(1, radix)])
        reach *= radix
    return rounds


class Stage:
    shapes = (
        ((LANES, ROWS), F32),
        ((16, WIDTH), BF16),
        ((16, WIDTH), BF16),
        ((ROWS, LANES), F32),
        ((ROWS, LANES), F32),
        ((WIDTH, WIDTH), BF16),
        ((WIDTH, WIDTH), BF16),
        ((16, WIDTH), BF16),
        ((16, WIDTH), BF16),
        ((ROWS, LANES), F32),
        ((ROWS, LANES), F32),
    )

    def __init__(self, refs):
        (self.columns, self.w_owner, self.w_partner,
         self.s_owner, self.s_partner, self.high, self.low,
         self.held_w_owner, self.held_w_partner, self.held_s_owner, self.held_s_partner) = refs

    def prepare(self, first, second):
        corner = jnp.broadcast_to(first[:, 0:1], (ROWS, LANES))
        centre = in_halves(corner, pltpu.roll(corner, 4, 0))
        place_first, self.w_owner[...] = weights(first, centre)
        place_second, self.w_partner[...] = weights(second, centre)
        self.s_owner[...] = place_first
        self.s_partner[...] = place_second
        self.columns[...] = jnp.transpose(place_first)

    def strengths(self):
        second = self.s_partner[...]
        self.held_w_owner[...] = self.w_owner[...]
        self.held_w_partner[...] = self.w_partner[...]
        self.held_s_owner[...] = self.s_owner[...]
        self.held_s_partner[...] = second
        for top in range(0, WIDTH, BLOCK):
            rows = slice(top, top + BLOCK)
            half, top = divmod(top, LANES)
            xi = [
                jnp.broadcast_to(self.columns[top : top + BLOCK, at : at + 1], (BLOCK, LANES))
                for at in range(half * 4, half * 4 + 3)
            ]
            for side in range(2):
                xj = [jnp.broadcast_to(second[side * 4 + c : side * 4 + c + 1], (BLOCK, LANES)) for c in range(3)]
                strength = pair_strength(xi, xj)
                part = strength.astype(BF16)
                lanes = slice(side * LANES, (side + 1) * LANES)
                self.high[rows, lanes] = part
                self.low[rows, lanes] = (strength - part.astype(F32)).astype(BF16)

    def sums(self):
        plain = (((1,), (0,)), ((), ()))
        turned = (((1,), (1,)), ((), ()))
        wo, wp, high, low = self.held_w_owner[...], self.held_w_partner[...], self.high[...], self.low[...]
        to_partner = lax.dot_general(wo, high, plain, preferred_element_type=F32) + lax.dot_general(
            wo, low, plain, preferred_element_type=F32
        )
        to_owner = lax.dot_general(wp, high, turned, preferred_element_type=F32) + lax.dot_general(
            wp, low, turned, preferred_element_type=F32
        )
        return force(to_partner, self.held_s_partner[...]), force(to_owner, self.held_s_owner[...])


def forces_kernel(n_region, n_local, leaves, pairs, count, total, over,
                  out_msg, out_meta, msg, meta, partners, named, on_partner, on_owner, landed,
                  flag_out, flag_in, firsts, seconds, to_partners, to_owners,
                  msg_send, msg_recv, meta_send, meta_recv, back_send, back_recv, flag_send, flag_recv,
                  *stage_refs):
    here_region = lax.axis_index("region")
    here_local = lax.axis_index("local")
    n_leaf = leaves.shape[0] // ROWS
    n_pair = pairs.shape[1]
    n_seat = SHARDS * SEATS
    rounds = flag_rounds(n_region * n_local)
    strides = [stride for each in rounds for stride in each]
    per = len(Stage.shapes)
    stages = [Stage(stage_refs[i * per : (i + 1) * per]) for i in range(SLOTS)]
    last = (((1,), (1,)), ((), ()))

    def device(hop, offset):
        return (
            lax.rem(here_region + hop + n_region, n_region),
            lax.rem(here_local + offset + n_local, n_local),
        )

    def partner_device(h):
        return device(h // 5, h % 5 - 2)

    def lister_device(h):
        return device(-(h // 5), 2 - h % 5)

    barrier = pltpu.get_barrier_semaphore()
    friends = []
    for h in range(SHARDS):
        if h != OWN:
            friends += [(h // 5, h % 5 - 2), (-(h // 5), 2 - h % 5)]
    for stride in strides:
        friend = (-(stride // n_local), -(stride % n_local))
        if friend not in friends:
            friends.append(friend)
    for friend in friends:
        pl.semaphore_signal(barrier, inc=1, device_id=device(*friend), device_id_type=MESH)

    owner = pairs[0:1, :]
    index = pairs[1:2, :]
    shard = index // 64
    leaf = index % 64
    live = lax.broadcasted_iota(I32, (1, n_pair), 1) < count[0:1, 0:1]
    member = ((lax.broadcasted_iota(I32, (16, n_pair), 0) == shard) & live).astype(F32)
    before = lax.broadcasted_iota(I32, (n_pair, n_pair), 0) < lax.broadcasted_iota(I32, (n_pair, n_pair), 1)
    ahead = jnp.dot(member.astype(BF16), before.astype(F32).astype(BF16), preferred_element_type=F32)
    rank = jnp.sum(member * ahead, axis=0, keepdims=True).astype(I32)
    seat = jnp.where(live & (rank < SLOTS), shard * SEATS + rank, -1)
    flag_out[0] = jnp.broadcast_to(
        jnp.max(jnp.where(live & (rank >= SLOTS), 1, 0), axis=1, keepdims=True), (8, LANES)
    )
    seated = (lax.broadcasted_iota(I32, (n_seat, n_pair), 0) == seat).astype(F32).astype(BF16)
    owned = (lax.broadcasted_iota(I32, (n_leaf, n_pair), 0) == owner).astype(F32).astype(BF16)
    choice = lax.dot_general(seated, owned, last, preferred_element_type=F32).astype(BF16)
    back = lax.dot_general(owned, seated, last, preferred_element_type=F32).astype(BF16)
    names = jnp.broadcast_to((leaf + 1).astype(F32), (LANES, n_pair)).astype(BF16)
    partner = lax.dot_general(seated, names, last, preferred_element_type=F32).astype(I32) - 1
    for h in range(SHARDS):
        out_meta[h] = partner[h * SEATS : (h + 1) * SEATS, :]
    for row in range(ROWS):
        plane = picked(choice, leaves[pl.ds(row, n_leaf, stride=ROWS), :])
        for h in range(SHARDS):
            out_msg[h, row * SEATS : (row + 1) * SEATS, :] = plane[h * SEATS : (h + 1) * SEATS, :]

    def message(h):
        return pltpu.make_async_remote_copy(
            src_ref=out_msg.at[h], dst_ref=msg.at[h], send_sem=msg_send.at[h], recv_sem=msg_recv.at[h],
            device_id=partner_device(h), device_id_type=MESH,
        )

    def names_of(h):
        return pltpu.make_async_remote_copy(
            src_ref=out_meta.at[h], dst_ref=meta.at[h], send_sem=meta_send.at[h], recv_sem=meta_recv.at[h],
            device_id=partner_device(h), device_id_type=MESH,
        )

    def answer(h):
        return pltpu.make_async_remote_copy(
            src_ref=on_owner.at[h], dst_ref=landed.at[h], send_sem=back_send.at[h], recv_sem=back_recv.at[h],
            device_id=lister_device(h), device_id_type=MESH,
        )

    def flag(step, stride):
        lane = strides.index(stride)
        return pltpu.make_async_remote_copy(
            src_ref=flag_out.at[step], dst_ref=flag_in.at[lane],
            send_sem=flag_send.at[lane], recv_sem=flag_recv.at[lane],
            device_id=device(stride // n_local, stride % n_local), device_id_type=MESH,
        )

    pl.semaphore_wait(barrier, len(friends))
    others = [(OWN + place) % SHARDS for place in range(1, SHARDS)]
    for h in others:
        names_of(h).start()
    for h in others:
        message(h).start()
    for stride in rounds[0]:
        flag(0, stride).start()

    to_partners[...] = jnp.zeros_like(to_partners)
    to_owners[...] = jnp.zeros_like(to_owners)
    msg[OWN] = out_msg[OWN]
    meta[OWN] = out_meta[OWN]

    def gather(shards_here):
        rows = len(shards_here) * SEATS
        seats = jnp.concatenate([meta[h] for h in shards_here], axis=0)
        wanted = (seats == lax.broadcasted_iota(I32, (rows, LANES), 1)).astype(F32).astype(BF16)
        for place, h in enumerate(shards_here):
            named[h] = wanted[place * SEATS : (place + 1) * SEATS].astype(F32)
        for row in range(ROWS):
            plane = picked(wanted[:, :n_leaf], leaves[pl.ds(row, n_leaf, stride=ROWS), :])
            for place, h in enumerate(shards_here):
                partners[h, row * SEATS : (row + 1) * SEATS, :] = plane[place * SEATS : (place + 1) * SEATS, :]

    def prepare(h):
        firsts[...] = msg[h]
        seconds[...] = partners[h]

    def prepare_slot(slot):
        seat_rows = pl.ds(slot, ROWS, stride=SEATS)
        stages[slot].prepare(firsts[seat_rows, :], seconds[seat_rows, :])

    def finish_slot(slot):
        seat_rows = pl.ds(slot, ROWS, stride=SEATS)
        to_partners[seat_rows, :], to_owners[seat_rows, :] = stages[slot].sums()

    def finish(h):
        on_partner[h] = to_partners[...]
        on_owner[h] = to_owners[...]

    turned = (here_local == 0) * 2 + (here_local == 1) * 1
    turned = turned + (here_local == n_local - 1) * 3 + (here_local == n_local - 2) * 4
    own_turn = 2 * ((7 - turned) % 5)

    def shard_at(place):
        turn = place + (place >= own_turn) * 1
        return turn % 2 * 5 + 4 - (turn // 2 + turned) % 5

    gather([OWN])
    prepare(OWN)
    for slot in range(SLOTS):
        prepare_slot(slot)
    for slot in range(SLOTS):
        stages[slot].strengths()
    for h in others:
        names_of(h).wait_recv()
    gather(others)
    first_shard = shard_at(jnp.int32(0))
    message(first_shard).wait_recv()
    prepare(first_shard)
    for slot in range(SLOTS):
        prepare_slot(slot)

    def turn(place, h_before):
        h = shard_at(place - 1)
        h_next = shard_at(jnp.minimum(place, SHARDS - 2))

        @pl.when(place < SHARDS - 1)
        def _():
            message(h_next).wait_recv()

        for step, each in enumerate(rounds):

            @pl.when(place == SHARDS - 1 - 2 * (len(rounds) - 1 - step))
            def _(step=step, each=each):
                heard = flag_out[step]
                for stride in each:
                    flag(step, stride).wait()
                    heard = jnp.maximum(heard, flag_in[strides.index(stride)])
                flag_out[step + 1] = heard
                if step + 1 < len(rounds):
                    for stride in rounds[step + 1]:
                        flag(step + 1, stride).start()

        prepare(h_next)
        for slot in range(SLOTS):
            finish_slot(slot)
            stages[slot].strengths()
            prepare_slot(slot)
        finish(h_before)

        @pl.when(place >= 2)
        def _():
            answer(h_before).start()

        return h

    h_end = lax.fori_loop(1, SHARDS, turn, jnp.int32(OWN))
    for slot in range(SLOTS):
        finish_slot(slot)
    finish(h_end)
    answer(h_end).start()
    over[...] = flag_out[len(rounds)]
    for h in others:
        names_of(h).wait_send()
        message(h).wait_send()
    for h in others:
        answer(h).wait()

    wanted = jnp.concatenate([named[h] for h in range(SHARDS)], axis=0).astype(BF16)
    first = (((0,), (0,)), ((), ()))
    for half in range(2):
        for c in range(3):
            rows = slice((half * 4 + c) * SEATS, (half * 4 + c + 1) * SEATS)
            listed = jnp.concatenate(
                [(on_owner if h == OWN else landed)[h, rows, :] for h in range(SHARDS)], axis=0
            )
            met = jnp.concatenate([on_partner[h, rows, :] for h in range(SHARDS)], axis=0)
            result = None
            for part, other in zip(thirds(listed)[::-1], thirds(met)[::-1]):
                term = jnp.dot(back, part, preferred_element_type=F32) + lax.dot_general(
                    wanted, other, first, preferred_element_type=F32
                )[:n_leaf]
                result = term if result is None else result + term
            total[c, :, half * LANES : (half + 1) * LANES] = result


def forces(leaves, pairs, count, n_region, n_local):
    vmem = pl.BlockSpec(memory_space=pltpu.VMEM)
    n_leaf = leaves.shape[0] // ROWS
    rounds = flag_rounds(n_region * n_local)
    n_flag = sum(len(each) for each in rounds)
    message = pltpu.VMEM((SHARDS, ROWS * SEATS, LANES), F32)
    names = pltpu.VMEM((SHARDS, SEATS, LANES), I32)

    def kernel(*refs):
        forces_kernel(n_region, n_local, *refs)

    return pl.pallas_call(
        kernel,
        out_shape=(
            jax.ShapeDtypeStruct((3, n_leaf, WIDTH), F32),
            jax.ShapeDtypeStruct((8, LANES), I32),
        ),
        in_specs=[vmem, vmem, vmem],
        out_specs=(vmem, vmem),
        scratch_shapes=[
            message,
            names,
            message,
            names,
            message,
            pltpu.VMEM((SHARDS, SEATS, LANES), F32),
            message,
            message,
            message,
            pltpu.VMEM((len(rounds) + 1, 8, LANES), I32),
            pltpu.VMEM((n_flag, 8, LANES), I32),
        ]
        + [pltpu.VMEM((ROWS * SEATS, LANES), F32)] * 4
        + [pltpu.SemaphoreType.DMA((SHARDS,))] * 6
        + [pltpu.SemaphoreType.DMA((n_flag,))] * 2
        + [pltpu.VMEM(*shape) for shape in Stage.shapes] * SLOTS,
        compiler_params=pltpu.CompilerParams(
            collective_id=0, has_side_effects=True, vmem_limit_bytes=32 * 2**20
        ),
        name="forces",
    )(leaves, pairs, count)


def passed_along(value, axis, steps):
    if steps == 0:
        return value
    count = lax.axis_size(axis)
    pairs = [(source, (source + steps) % count) for source in range(count)]
    return lax.ppermute(value, axis, pairs)


def dense_pair(first, second):
    dx = second[:3, None, :] - first[:3, :, None]
    r2 = jnp.sum(dx * dx, axis=0) + 0.09
    dist = jnp.sqrt(r2)
    kern = (lax.erfc(dist * 0.5) + dist * INV_SQRT_PI * jnp.exp(-r2 * 0.25)) / (r2 * dist)
    weighted = dx * kern[None, :, :]
    on_first = jnp.sum(weighted * second[3][None, None, :], axis=2)
    on_second = -jnp.sum(weighted * first[3][None, :, None], axis=1)
    return (on_first, on_second)


def by_windows(positions, pair_list, pair_count):
    leaf_dev, _, width = positions.shape
    offsets = (-2, -1, 0, 1, 2)
    here = jnp.concatenate([passed_along(positions, "local", -offset) for offset in offsets], axis=0)
    table = jnp.concatenate([here, passed_along(here, "region", -1)], axis=0)
    span = here.shape[0]
    slots = pair_list.shape[0]
    alive = (jnp.arange(slots, dtype=I32) < pair_count[0]).astype(F32)

    def step(carry, inputs):
        own_part, react_part = carry
        pair, weight = inputs
        on_first, on_second = dense_pair(positions[pair[0]], table[pair[1]])
        own_part = own_part.at[pair[0]].add(on_first * weight)
        react_part = react_part.at[pair[1]].add(on_second * weight)
        return ((own_part, react_part), None)

    own_part = jnp.zeros((leaf_dev, 3, width), F32)
    reaction = jnp.zeros((2 * span, 3, width), F32)
    (own_part, reaction), _ = lax.scan(step, (own_part, reaction), (pair_list, alive))
    reaction = reaction[:span] + passed_along(reaction[span:], "region", 1)
    for place, offset in enumerate(offsets):
        piece = reaction[place * leaf_dev : (place + 1) * leaf_dev]
        own_part = own_part + passed_along(piece, "local", offset)
    return own_part.transpose(1, 0, 2)


def shards(positions, pair_list, pair_count, active):
    n_region = lax.axis_size("region")
    n_local = lax.axis_size("local")
    n_leaf, n_row, width = positions.shape
    leaves = positions.reshape(n_leaf, n_row, 2, LANES).transpose(0, 2, 1, 3).reshape(n_leaf * ROWS, LANES)
    total, over = forces(leaves, pair_list.T, pair_count.reshape(1, 1), n_region, n_local)
    total = lax.cond(
        over[0, 0] > 0,
        lambda total: by_windows(positions, pair_list, pair_count),
        lambda total: total,
        total,
    )
    return (total * active.astype(F32)[None, :, None]).transpose(1, 0, 2)


def solution(mesh):
    return jax.shard_map(
        shards,
        mesh=mesh,
        in_specs=(
            P(("region", "local"), None, None),
            P(("region", "local"), None),
            P(("region", "local")),
            P(("region", "local")),
        ),
        out_specs=P(("region", "local"), None, None),
        check_vma=False,
    )
```

```python
import math

import jax
import jax.numpy as jnp
from jax import lax
from jax.experimental import pallas as pl
from jax.experimental.pallas import tpu as pltpu
from jax.sharding import PartitionSpec as P

F32 = jnp.float32
BF16 = jnp.bfloat16
I32 = jnp.int32
MESH = pl.DeviceIdType.MESH

SHARDS = 10
SEATS = 8
SLOTS = 7
ROWS = 8
LANES = 128
WIDTH = 2 * LANES
OWN = 2
BLOCK = 32

SHIFT = 0.25
ERFCX = (
    0.9999664993365988,
    -0.5639379807585301,
    0.10826155296772119,
    -0.0033908818915562877,
    -0.001816315565602909,
    0.00020140930421213982,
)
INV_SQRT_PI = 1.0 / math.sqrt(math.pi)

UNIT = math.sqrt(0.25 / math.log(2.0))
SOFTENING = 0.09 * UNIT**2
UNIT_SHIFT = SHIFT / UNIT
UNIT_ERFCX = tuple(c * UNIT ** (2 - n) for n, c in enumerate(ERFCX))
UNIT_TAIL = UNIT * INV_SQRT_PI


def thirds(value):
    high = value.astype(BF16)
    rest = value - high.astype(F32)
    middle = rest.astype(BF16)
    low = (rest - middle.astype(F32)).astype(BF16)
    return high, middle, low


def picked(choice, value):
    total = None
    for part in reversed(thirds(value)):
        term = jnp.dot(choice, part, preferred_element_type=F32)
        total = term if total is None else total + term
    return total


def pair_strength(first, second):
    dx = second[0] - first[0]
    dy = second[1] - first[1]
    dz = second[2] - first[2]
    r2 = dx * dx + dy * dy + (dz * dz + SOFTENING)
    inverse = lax.rsqrt(r2)
    near = pl.reciprocal(inverse + UNIT_SHIFT, approx=True)
    series = near * UNIT_ERFCX[-1] + UNIT_ERFCX[-2]
    for coefficient in UNIT_ERFCX[-3::-1]:
        series = series * near + coefficient
    return (series * inverse + UNIT_TAIL) * pl.reciprocal(r2 * jnp.exp2(r2), approx=True)


def in_halves(low_half, high_half):
    low = lax.broadcasted_iota(I32, (ROWS, LANES), 0) < 4
    return jnp.where(low, low_half, high_half)


def spread_rows(tile, row):
    return in_halves(
        jnp.broadcast_to(tile[row : row + 1], (ROWS, LANES)),
        jnp.broadcast_to(tile[row + 4 : row + 5], (ROWS, LANES)),
    )


def weights(tile, centre):
    row = lax.broadcasted_iota(I32, (ROWS, LANES), 0)
    shifted = (tile - centre) * UNIT
    mass = spread_rows(tile, 3)
    weighted = jnp.where(row % 4 == 3, mass, shifted * mass)
    a, b, c = (part.astype(F32) for part in thirds(weighted))
    a_up, b_up, c_up = (pltpu.roll(part, 4, 0) for part in (a, b, c))
    none = jnp.zeros_like(c)
    top = jnp.concatenate([in_halves(a, b_up), in_halves(a_up, b)], axis=1)
    bottom = jnp.concatenate([in_halves(c, none), in_halves(c_up, none)], axis=1)
    return shifted, jnp.concatenate([top, bottom], axis=0).astype(BF16)


def force(sums, shifted):
    top, bottom = sums[:8], sums[8:]
    joined = top + pltpu.roll(top, 4, 0) + bottom
    tile = in_halves(joined[:, :LANES], pltpu.roll(joined[:, LANES:], 4, 0))
    return tile - shifted * spread_rows(tile, 3)


def flag_rounds(n_device):
    rounds = []
    reach = 1
    while reach < n_device:
        radix = min(4, n_device // reach)
        rounds.append([reach * step for step in range(1, radix)])
        reach *= radix
    return rounds


class Stage:
    shapes = (
        ((LANES, ROWS), F32),
        ((16, WIDTH), BF16),
        ((16, WIDTH), BF16),
        ((ROWS, LANES), F32),
        ((ROWS, LANES), F32),
        ((WIDTH, WIDTH), BF16),
        ((WIDTH, WIDTH), BF16),
        ((16, WIDTH), BF16),
        ((16, WIDTH), BF16),
        ((ROWS, LANES), F32),
        ((ROWS, LANES), F32),
    )

    def __init__(self, refs):
        (self.columns, self.w_owner, self.w_partner,
         self.s_owner, self.s_partner, self.high, self.low,
         self.held_w_owner, self.held_w_partner, self.held_s_owner, self.held_s_partner) = refs

    def prepare(self, first, second):
        corner = jnp.broadcast_to(first[:, 0:1], (ROWS, LANES))
        centre = in_halves(corner, pltpu.roll(corner, 4, 0))
        place_first, self.w_owner[...] = weights(first, centre)
        place_second, self.w_partner[...] = weights(second, centre)
        self.s_owner[...] = place_first
        self.s_partner[...] = place_second
        self.columns[...] = jnp.transpose(place_first)

    def strengths(self):
        second = self.s_partner[...]
        self.held_w_owner[...] = self.w_owner[...]
        self.held_w_partner[...] = self.w_partner[...]
        self.held_s_owner[...] = self.s_owner[...]
        self.held_s_partner[...] = second
        for top in range(0, WIDTH, BLOCK):
            rows = slice(top, top + BLOCK)
            half, top = divmod(top, LANES)
            xi = [
                jnp.broadcast_to(self.columns[top : top + BLOCK, at : at + 1], (BLOCK, LANES))
                for at in range(half * 4, half * 4 + 3)
            ]
            for side in range(2):
                xj = [jnp.broadcast_to(second[side * 4 + c : side * 4 + c + 1], (BLOCK, LANES)) for c in range(3)]
                strength = pair_strength(xi, xj)
                part = strength.astype(BF16)
                lanes = slice(side * LANES, (side + 1) * LANES)
                self.high[rows, lanes] = part
                self.low[rows, lanes] = (strength - part.astype(F32)).astype(BF16)

    def sums(self):
        plain = (((1,), (0,)), ((), ()))
        turned = (((1,), (1,)), ((), ()))
        wo, wp, high, low = self.held_w_owner[...], self.held_w_partner[...], self.high[...], self.low[...]
        to_partner = lax.dot_general(wo, high, plain, preferred_element_type=F32) + lax.dot_general(
            wo, low, plain, preferred_element_type=F32
        )
        to_owner = lax.dot_general(wp, high, turned, preferred_element_type=F32) + lax.dot_general(
            wp, low, turned, preferred_element_type=F32
        )
        return force(to_partner, self.held_s_partner[...]), force(to_owner, self.held_s_owner[...])


def forces_kernel(n_region, n_local, leaves, pairs, count, active, total, over,
                  out_msg, out_meta, msg, meta, partners, named, on_partner, on_owner, landed,
                  flag_out, flag_in, firsts, seconds, to_partners, to_owners,
                  msg_send, msg_recv, meta_send, meta_recv, back_send, back_recv, flag_send, flag_recv,
                  *stage_refs):
    here_region = lax.axis_index("region")
    here_local = lax.axis_index("local")
    n_leaf = leaves.shape[0] // ROWS
    n_pair = pairs.shape[1]
    n_seat = SHARDS * SEATS
    rounds = flag_rounds(n_region * n_local)
    strides = [stride for each in rounds for stride in each]
    per = len(Stage.shapes)
    stages = [Stage(stage_refs[i * per : (i + 1) * per]) for i in range(SLOTS)]
    last = (((1,), (1,)), ((), ()))

    def device(hop, offset):
        return (
            lax.rem(here_region + hop + n_region, n_region),
            lax.rem(here_local + offset + n_local, n_local),
        )

    def partner_device(h):
        return device(h // 5, h % 5 - 2)

    def lister_device(h):
        return device(-(h // 5), 2 - h % 5)

    barrier = pltpu.get_barrier_semaphore()
    friends = []
    for h in range(SHARDS):
        if h != OWN:
            friends += [(h // 5, h % 5 - 2), (-(h // 5), 2 - h % 5)]
    for stride in strides:
        friend = (-(stride // n_local), -(stride % n_local))
        if friend not in friends:
            friends.append(friend)
    for friend in friends:
        pl.semaphore_signal(barrier, inc=1, device_id=device(*friend), device_id_type=MESH)

    owner = pairs[0:1, :]
    index = pairs[1:2, :]
    shard = index // 64
    leaf = index % 64
    live = lax.broadcasted_iota(I32, (1, n_pair), 1) < count[0:1, 0:1]
    member = ((lax.broadcasted_iota(I32, (16, n_pair), 0) == shard) & live).astype(F32)
    before = lax.broadcasted_iota(I32, (n_pair, n_pair), 0) < lax.broadcasted_iota(I32, (n_pair, n_pair), 1)
    ahead = jnp.dot(member.astype(BF16), before.astype(F32).astype(BF16), preferred_element_type=F32)
    rank = jnp.sum(member * ahead, axis=0, keepdims=True).astype(I32)
    seat = jnp.where(live & (rank < SLOTS), shard * SEATS + rank, -1)
    flag_out[0] = jnp.broadcast_to(
        jnp.max(jnp.where(live & (rank >= SLOTS), 1, 0), axis=1, keepdims=True), (8, LANES)
    )
    seated = (lax.broadcasted_iota(I32, (n_seat, n_pair), 0) == seat).astype(F32).astype(BF16)
    owned = (lax.broadcasted_iota(I32, (n_leaf, n_pair), 0) == owner).astype(F32).astype(BF16)
    choice = lax.dot_general(seated, owned, last, preferred_element_type=F32).astype(BF16)
    back = lax.dot_general(owned, seated, last, preferred_element_type=F32).astype(BF16)
    square = lax.broadcasted_iota(I32, (n_leaf, n_leaf), 0) == lax.broadcasted_iota(I32, (n_leaf, n_leaf), 1)
    kept = jnp.where(square, jnp.broadcast_to(active[...].astype(F32), (n_leaf, n_leaf)), 0.0).astype(BF16)
    back = jnp.dot(kept, back, preferred_element_type=F32).astype(BF16)
    names = jnp.broadcast_to((leaf + 1).astype(F32), (LANES, n_pair)).astype(BF16)
    partner = lax.dot_general(seated, names, last, preferred_element_type=F32).astype(I32) - 1
    for h in range(SHARDS):
        out_meta[h] = partner[h * SEATS : (h + 1) * SEATS, :]
    for row in range(ROWS):
        plane = picked(choice, leaves[pl.ds(row, n_leaf, stride=ROWS), :])
        for h in range(SHARDS):
            out_msg[h, row * SEATS : (row + 1) * SEATS, :] = plane[h * SEATS : (h + 1) * SEATS, :]

    def message(h):
        return pltpu.make_async_remote_copy(
            src_ref=out_msg.at[h], dst_ref=msg.at[h], send_sem=msg_send.at[h], recv_sem=msg_recv.at[h],
            device_id=partner_device(h), device_id_type=MESH,
        )

    def names_of(h):
        return pltpu.make_async_remote_copy(
            src_ref=out_meta.at[h], dst_ref=meta.at[h], send_sem=meta_send.at[h], recv_sem=meta_recv.at[h],
            device_id=partner_device(h), device_id_type=MESH,
        )

    def answer(h):
        return pltpu.make_async_remote_copy(
            src_ref=on_owner.at[h], dst_ref=landed.at[h], send_sem=back_send.at[h], recv_sem=back_recv.at[h],
            device_id=lister_device(h), device_id_type=MESH,
        )

    def flag(step, stride):
        lane = strides.index(stride)
        return pltpu.make_async_remote_copy(
            src_ref=flag_out.at[step], dst_ref=flag_in.at[lane],
            send_sem=flag_send.at[lane], recv_sem=flag_recv.at[lane],
            device_id=device(stride // n_local, stride % n_local), device_id_type=MESH,
        )

    pl.semaphore_wait(barrier, len(friends))
    others = [(OWN + place) % SHARDS for place in range(1, SHARDS)]
    for h in others:
        names_of(h).start()
    for h in others:
        message(h).start()
    for stride in rounds[0]:
        flag(0, stride).start()

    to_partners[...] = jnp.zeros_like(to_partners)
    to_owners[...] = jnp.zeros_like(to_owners)
    msg[OWN] = out_msg[OWN]
    meta[OWN] = out_meta[OWN]

    def gather(shards_here):
        rows = len(shards_here) * SEATS
        seats = jnp.concatenate([meta[h] for h in shards_here], axis=0)
        wanted = (seats == lax.broadcasted_iota(I32, (rows, LANES), 1)).astype(F32).astype(BF16)
        for place, h in enumerate(shards_here):
            named[h] = wanted[place * SEATS : (place + 1) * SEATS].astype(F32)
        for row in range(ROWS):
            plane = picked(wanted[:, :n_leaf], leaves[pl.ds(row, n_leaf, stride=ROWS), :])
            for place, h in enumerate(shards_here):
                partners[h, row * SEATS : (row + 1) * SEATS, :] = plane[place * SEATS : (place + 1) * SEATS, :]

    def prepare(h):
        firsts[...] = msg[h]
        seconds[...] = partners[h]

    def prepare_slot(slot):
        seat_rows = pl.ds(slot, ROWS, stride=SEATS)
        stages[slot].prepare(firsts[seat_rows, :], seconds[seat_rows, :])

    def finish_slot(slot):
        seat_rows = pl.ds(slot, ROWS, stride=SEATS)
        to_partners[seat_rows, :], to_owners[seat_rows, :] = stages[slot].sums()

    def finish(h):
        on_partner[h] = to_partners[...]
        on_owner[h] = to_owners[...]

    turned = (here_local == 0) * 2 + (here_local == 1) * 1
    turned = turned + (here_local == n_local - 1) * 3 + (here_local == n_local - 2) * 4
    own_turn = 2 * ((7 - turned) % 5)

    def shard_at(place):
        turn = place + (place >= own_turn) * 1
        return turn % 2 * 5 + 4 - (turn // 2 + turned) % 5

    gather([OWN])
    prepare(OWN)
    for slot in range(SLOTS):
        prepare_slot(slot)
    for slot in range(SLOTS):
        stages[slot].strengths()

    def gather_places(group):
        met_here = [shard_at(jnp.int32(place)) for place in group]
        for h in met_here:
            names_of(h).wait_recv()
        gather(met_here)

    groups = ((0, 1, 2), (3, 4, 5), (6, 7, 8))
    gather_places(groups[0])
    first_shard = shard_at(jnp.int32(0))
    message(first_shard).wait_recv()
    prepare(first_shard)
    for slot in range(SLOTS):
        prepare_slot(slot)

    def turn(place, h_before):
        h = shard_at(place - 1)
        h_next = shard_at(jnp.minimum(place, SHARDS - 2))

        @pl.when(place < SHARDS - 1)
        def _():
            message(h_next).wait_recv()

        for group in groups[1:]:

            @pl.when(place == group[0])
            def _(group=group):
                gather_places(group)

        for step, each in enumerate(rounds):

            @pl.when(place == SHARDS - 1 - 2 * (len(rounds) - 1 - step))
            def _(step=step, each=each):
                heard = flag_out[step]
                for stride in each:
                    flag(step, stride).wait()
                    heard = jnp.maximum(heard, flag_in[strides.index(stride)])
                flag_out[step + 1] = heard
                if step + 1 < len(rounds):
                    for stride in rounds[step + 1]:
                        flag(step + 1, stride).start()

        prepare(h_next)
        for slot in range(SLOTS):
            finish_slot(slot)
            stages[slot].strengths()
            prepare_slot(slot)
        finish(h_before)

        @pl.when(place >= 2)
        def _():
            answer(h_before).start()

        return h

    h_end = lax.fori_loop(1, SHARDS, turn, jnp.int32(OWN))
    for slot in range(SLOTS):
        finish_slot(slot)
    finish(h_end)
    answer(h_end).start()
    over[...] = flag_out[len(rounds)]
    for h in others:
        names_of(h).wait_send()
        message(h).wait_send()

    def planes(sources):
        for half in range(2):
            for c in range(3):
                rows = slice((half * 4 + c) * SEATS, (half * 4 + c + 1) * SEATS)
                yield c, slice(half * LANES, (half + 1) * LANES), jnp.concatenate(
                    [source[h, rows, :] for h, source in enumerate(sources)], axis=0
                )

    wanted = jnp.concatenate([named[h] for h in range(SHARDS)], axis=0).astype(BF16)[:, :n_leaf]
    met = lax.dot_general(kept, wanted, last, preferred_element_type=F32).astype(BF16)
    for c, lanes, forces_met in planes([on_partner] * SHARDS):
        total[c, :, lanes] = picked(met, forces_met)
    for h in others:
        answer(h).wait()
    for c, lanes, forces_listed in planes([on_owner if h == OWN else landed for h in range(SHARDS)]):
        total[c, :, lanes] = total[c, :, lanes] + picked(back, forces_listed)


def forces(leaves, pairs, count, active, n_region, n_local):
    vmem = pl.BlockSpec(memory_space=pltpu.VMEM)
    n_leaf = leaves.shape[0] // ROWS
    rounds = flag_rounds(n_region * n_local)
    n_flag = sum(len(each) for each in rounds)
    message = pltpu.VMEM((SHARDS, ROWS * SEATS, LANES), F32)
    names = pltpu.VMEM((SHARDS, SEATS, LANES), I32)

    def kernel(*refs):
        forces_kernel(n_region, n_local, *refs)

    return pl.pallas_call(
        kernel,
        out_shape=(
            jax.ShapeDtypeStruct((3, n_leaf, WIDTH), F32),
            jax.ShapeDtypeStruct((8, LANES), I32),
        ),
        in_specs=[vmem, vmem, vmem, vmem],
        out_specs=(vmem, vmem),
        scratch_shapes=[
            message,
            names,
            message,
            names,
            message,
            pltpu.VMEM((SHARDS, SEATS, LANES), F32),
            message,
            message,
            message,
            pltpu.VMEM((len(rounds) + 1, 8, LANES), I32),
            pltpu.VMEM((n_flag, 8, LANES), I32),
        ]
        + [pltpu.VMEM((ROWS * SEATS, LANES), F32)] * 4
        + [pltpu.SemaphoreType.DMA((SHARDS,))] * 6
        + [pltpu.SemaphoreType.DMA((n_flag,))] * 2
        + [pltpu.VMEM(*shape) for shape in Stage.shapes] * SLOTS,
        compiler_params=pltpu.CompilerParams(
            collective_id=0, has_side_effects=True, vmem_limit_bytes=32 * 2**20
        ),
        name="forces",
    )(leaves, pairs, count, active)


def passed_along(value, axis, steps):
    if steps == 0:
        return value
    count = lax.axis_size(axis)
    pairs = [(source, (source + steps) % count) for source in range(count)]
    return lax.ppermute(value, axis, pairs)


def dense_pair(first, second):
    dx = second[:3, None, :] - first[:3, :, None]
    r2 = jnp.sum(dx * dx, axis=0) + 0.09
    dist = jnp.sqrt(r2)
    kern = (lax.erfc(dist * 0.5) + dist * INV_SQRT_PI * jnp.exp(-r2 * 0.25)) / (r2 * dist)
    weighted = dx * kern[None, :, :]
    on_first = jnp.sum(weighted * second[3][None, None, :], axis=2)
    on_second = -jnp.sum(weighted * first[3][None, :, None], axis=1)
    return (on_first, on_second)


def by_windows(positions, pair_list, pair_count):
    leaf_dev, _, width = positions.shape
    offsets = (-2, -1, 0, 1, 2)
    here = jnp.concatenate([passed_along(positions, "local", -offset) for offset in offsets], axis=0)
    table = jnp.concatenate([here, passed_along(here, "region", -1)], axis=0)
    span = here.shape[0]
    slots = pair_list.shape[0]
    alive = (jnp.arange(slots, dtype=I32) < pair_count[0]).astype(F32)

    def step(carry, inputs):
        own_part, react_part = carry
        pair, weight = inputs
        on_first, on_second = dense_pair(positions[pair[0]], table[pair[1]])
        own_part = own_part.at[pair[0]].add(on_first * weight)
        react_part = react_part.at[pair[1]].add(on_second * weight)
        return ((own_part, react_part), None)

    own_part = jnp.zeros((leaf_dev, 3, width), F32)
    reaction = jnp.zeros((2 * span, 3, width), F32)
    (own_part, reaction), _ = lax.scan(step, (own_part, reaction), (pair_list, alive))
    reaction = reaction[:span] + passed_along(reaction[span:], "region", 1)
    for place, offset in enumerate(offsets):
        piece = reaction[place * leaf_dev : (place + 1) * leaf_dev]
        own_part = own_part + passed_along(piece, "local", offset)
    return own_part.transpose(1, 0, 2)


def shards(positions, pair_list, pair_count, active):
    n_region = lax.axis_size("region")
    n_local = lax.axis_size("local")
    n_leaf, n_row, width = positions.shape
    leaves = positions.reshape(n_leaf, n_row, 2, LANES).transpose(0, 2, 1, 3).reshape(n_leaf * ROWS, LANES)
    total, over = forces(
        leaves, pair_list.T, pair_count.reshape(1, 1), active.reshape(1, n_leaf), n_region, n_local
    )
    total = lax.cond(
        over[0, 0] > 0,
        lambda total: by_windows(positions, pair_list, pair_count) * active.astype(F32)[None, :, None],
        lambda total: total,
        total,
    )
    return total.transpose(1, 0, 2)


def solution(mesh):
    return jax.shard_map(
        shards,
        mesh=mesh,
        in_specs=(
            P(("region", "local"), None, None),
            P(("region", "local"), None),
            P(("region", "local")),
            P(("region", "local")),
        ),
        out_specs=P(("region", "local"), None, None),
        check_vma=False,
    )
```

```python
import math

import jax
import jax.numpy as jnp
from jax import lax
from jax.experimental import pallas as pl
from jax.experimental.pallas import tpu as pltpu
from jax.sharding import PartitionSpec as P

F32 = jnp.float32
BF16 = jnp.bfloat16
I32 = jnp.int32
MESH = pl.DeviceIdType.MESH

SHARDS = 10
SEATS = 8
SLOTS = 7
ROWS = 8
LANES = 128
WIDTH = 2 * LANES
OWN = 2
BLOCK = 32

SHIFT = 0.25
ERFCX = (
    0.9999664993365988,
    -0.5639379807585301,
    0.10826155296772119,
    -0.0033908818915562877,
    -0.001816315565602909,
    0.00020140930421213982,
)
INV_SQRT_PI = 1.0 / math.sqrt(math.pi)

UNIT = math.sqrt(0.25 / math.log(2.0))
SOFTENING = 0.09 * UNIT**2
UNIT_SHIFT = SHIFT / UNIT
UNIT_ERFCX = tuple(c * UNIT ** (2 - n) for n, c in enumerate(ERFCX))
UNIT_TAIL = UNIT * INV_SQRT_PI


def thirds(value):
    high = value.astype(BF16)
    rest = value - high.astype(F32)
    middle = rest.astype(BF16)
    low = (rest - middle.astype(F32)).astype(BF16)
    return high, middle, low


def picked(choice, value):
    total = None
    for part in reversed(thirds(value)):
        term = jnp.dot(choice, part, preferred_element_type=F32)
        total = term if total is None else total + term
    return total


def pair_strength(first, second):
    dx = second[0] - first[0]
    dy = second[1] - first[1]
    dz = second[2] - first[2]
    r2 = dx * dx + dy * dy + (dz * dz + SOFTENING)
    inverse = lax.rsqrt(r2)
    near = pl.reciprocal(inverse + UNIT_SHIFT, approx=True)
    series = near * UNIT_ERFCX[-1] + UNIT_ERFCX[-2]
    for coefficient in UNIT_ERFCX[-3::-1]:
        series = series * near + coefficient
    return (series * inverse + UNIT_TAIL) * pl.reciprocal(r2 * jnp.exp2(r2), approx=True)


def in_halves(low_half, high_half):
    low = lax.broadcasted_iota(I32, (ROWS, LANES), 0) < 4
    return jnp.where(low, low_half, high_half)


def spread_rows(tile, row):
    return in_halves(
        jnp.broadcast_to(tile[row : row + 1], (ROWS, LANES)),
        jnp.broadcast_to(tile[row + 4 : row + 5], (ROWS, LANES)),
    )


def weights(tile, centre):
    row = lax.broadcasted_iota(I32, (ROWS, LANES), 0)
    shifted = (tile - centre) * UNIT
    mass = spread_rows(tile, 3)
    weighted = jnp.where(row % 4 == 3, mass, shifted * mass)
    a, b, c = (part.astype(F32) for part in thirds(weighted))
    a_up, b_up, c_up = (pltpu.roll(part, 4, 0) for part in (a, b, c))
    none = jnp.zeros_like(c)
    top = jnp.concatenate([in_halves(a, b_up), in_halves(a_up, b)], axis=1)
    bottom = jnp.concatenate([in_halves(c, none), in_halves(c_up, none)], axis=1)
    return shifted, jnp.concatenate([top, bottom], axis=0).astype(BF16)


def force(sums, shifted):
    top, bottom = sums[:8], sums[8:]
    joined = top + pltpu.roll(top, 4, 0) + bottom
    tile = in_halves(joined[:, :LANES], pltpu.roll(joined[:, LANES:], 4, 0))
    return tile - shifted * spread_rows(tile, 3)


def flag_rounds(n_device):
    rounds = []
    reach = 1
    while reach < n_device:
        radix = min(8 if reach == 1 else 4, n_device // reach)
        rounds.append([reach * step for step in range(1, radix)])
        reach *= radix
    return rounds


class Stage:
    shapes = (
        ((LANES, ROWS), F32),
        ((16, WIDTH), BF16),
        ((16, WIDTH), BF16),
        ((ROWS, LANES), F32),
        ((ROWS, LANES), F32),
        ((WIDTH, WIDTH), BF16),
        ((WIDTH, WIDTH), BF16),
        ((16, WIDTH), BF16),
        ((16, WIDTH), BF16),
        ((ROWS, LANES), F32),
        ((ROWS, LANES), F32),
    )

    def __init__(self, refs):
        (self.columns, self.w_owner, self.w_partner,
         self.s_owner, self.s_partner, self.high, self.low,
         self.held_w_owner, self.held_w_partner, self.held_s_owner, self.held_s_partner) = refs

    def prepare(self, first, second):
        corner = jnp.broadcast_to(first[:, 0:1], (ROWS, LANES))
        centre = in_halves(corner, pltpu.roll(corner, 4, 0))
        place_first, self.w_owner[...] = weights(first, centre)
        place_second, self.w_partner[...] = weights(second, centre)
        self.s_owner[...] = place_first
        self.s_partner[...] = place_second
        self.columns[...] = jnp.transpose(place_first)

    def strengths(self):
        second = self.s_partner[...]
        self.held_w_owner[...] = self.w_owner[...]
        self.held_w_partner[...] = self.w_partner[...]
        self.held_s_owner[...] = self.s_owner[...]
        self.held_s_partner[...] = second
        for top in range(0, WIDTH, BLOCK):
            rows = slice(top, top + BLOCK)
            half, top = divmod(top, LANES)
            xi = [
                jnp.broadcast_to(self.columns[top : top + BLOCK, at : at + 1], (BLOCK, LANES))
                for at in range(half * 4, half * 4 + 3)
            ]
            for side in range(2):
                xj = [jnp.broadcast_to(second[side * 4 + c : side * 4 + c + 1], (BLOCK, LANES)) for c in range(3)]
                strength = pair_strength(xi, xj)
                part = strength.astype(BF16)
                lanes = slice(side * LANES, (side + 1) * LANES)
                self.high[rows, lanes] = part
                self.low[rows, lanes] = (strength - part.astype(F32)).astype(BF16)

    def sums(self):
        plain = (((1,), (0,)), ((), ()))
        turned = (((1,), (1,)), ((), ()))
        wo, wp, high, low = self.held_w_owner[...], self.held_w_partner[...], self.high[...], self.low[...]
        to_partner = lax.dot_general(wo, high, plain, preferred_element_type=F32) + lax.dot_general(
            wo, low, plain, preferred_element_type=F32
        )
        to_owner = lax.dot_general(wp, high, turned, preferred_element_type=F32) + lax.dot_general(
            wp, low, turned, preferred_element_type=F32
        )
        return force(to_partner, self.held_s_partner[...]), force(to_owner, self.held_s_owner[...])


def forces_kernel(n_region, n_local, leaves, pairs, count, active, total, over,
                  out_msg, out_meta, msg, meta, partners, named, on_partner, on_owner, landed,
                  flag_out, flag_in, firsts, seconds, to_partners, to_owners,
                  msg_send, msg_recv, meta_send, meta_recv, back_send, back_recv, flag_send, flag_recv,
                  *stage_refs):
    here_region = lax.axis_index("region")
    here_local = lax.axis_index("local")
    n_leaf = leaves.shape[0] // ROWS
    n_pair = pairs.shape[1]
    n_seat = SHARDS * SEATS
    rounds = flag_rounds(n_region * n_local)
    strides = [stride for each in rounds for stride in each]
    per = len(Stage.shapes)
    stages = [Stage(stage_refs[i * per : (i + 1) * per]) for i in range(SLOTS)]
    last = (((1,), (1,)), ((), ()))

    def device(hop, offset):
        return (
            lax.rem(here_region + hop + n_region, n_region),
            lax.rem(here_local + offset + n_local, n_local),
        )

    def partner_device(h):
        return device(h // 5, h % 5 - 2)

    def lister_device(h):
        return device(-(h // 5), 2 - h % 5)

    barrier = pltpu.get_barrier_semaphore()
    friends = []
    for h in range(SHARDS):
        if h != OWN:
            friends += [(h // 5, h % 5 - 2), (-(h // 5), 2 - h % 5)]
    for stride in strides:
        friend = (-(stride // n_local), -(stride % n_local))
        if friend not in friends:
            friends.append(friend)
    for friend in friends:
        pl.semaphore_signal(barrier, inc=1, device_id=device(*friend), device_id_type=MESH)

    owner = pairs[0:1, :]
    index = pairs[1:2, :]
    shard = index // 64
    leaf = index % 64
    live = lax.broadcasted_iota(I32, (1, n_pair), 1) < count[0:1, 0:1]
    member = ((lax.broadcasted_iota(I32, (16, n_pair), 0) == shard) & live).astype(F32)
    before = lax.broadcasted_iota(I32, (n_pair, n_pair), 0) < lax.broadcasted_iota(I32, (n_pair, n_pair), 1)
    ahead = jnp.dot(member.astype(BF16), before.astype(F32).astype(BF16), preferred_element_type=F32)
    rank = jnp.sum(member * ahead, axis=0, keepdims=True).astype(I32)
    seat = jnp.where(live & (rank < SLOTS), shard * SEATS + rank, -1)
    flag_out[0] = jnp.broadcast_to(
        jnp.max(jnp.where(live & (rank >= SLOTS), 1, 0), axis=1, keepdims=True), (8, LANES)
    )
    seated = (lax.broadcasted_iota(I32, (n_seat, n_pair), 0) == seat).astype(F32).astype(BF16)
    owned = (lax.broadcasted_iota(I32, (n_leaf, n_pair), 0) == owner).astype(F32).astype(BF16)
    choice = lax.dot_general(seated, owned, last, preferred_element_type=F32).astype(BF16)
    back = lax.dot_general(owned, seated, last, preferred_element_type=F32).astype(BF16)
    square = lax.broadcasted_iota(I32, (n_leaf, n_leaf), 0) == lax.broadcasted_iota(I32, (n_leaf, n_leaf), 1)
    kept = jnp.where(square, jnp.broadcast_to(active[...].astype(F32), (n_leaf, n_leaf)), 0.0).astype(BF16)
    back = jnp.dot(kept, back, preferred_element_type=F32).astype(BF16)
    names = jnp.broadcast_to((leaf + 1).astype(F32), (LANES, n_pair)).astype(BF16)
    partner = lax.dot_general(seated, names, last, preferred_element_type=F32).astype(I32) - 1
    for h in range(SHARDS):
        out_meta[h] = partner[h * SEATS : (h + 1) * SEATS, :]
    for row in range(ROWS):
        plane = picked(choice, leaves[pl.ds(row, n_leaf, stride=ROWS), :])
        for h in range(SHARDS):
            out_msg[h, row * SEATS : (row + 1) * SEATS, :] = plane[h * SEATS : (h + 1) * SEATS, :]

    def message(h):
        return pltpu.make_async_remote_copy(
            src_ref=out_msg.at[h], dst_ref=msg.at[h], send_sem=msg_send.at[h], recv_sem=msg_recv.at[h],
            device_id=partner_device(h), device_id_type=MESH,
        )

    def names_of(h):
        return pltpu.make_async_remote_copy(
            src_ref=out_meta.at[h], dst_ref=meta.at[h], send_sem=meta_send.at[h], recv_sem=meta_recv.at[h],
            device_id=partner_device(h), device_id_type=MESH,
        )

    def answer(h):
        return pltpu.make_async_remote_copy(
            src_ref=on_owner.at[h], dst_ref=landed.at[h], send_sem=back_send.at[h], recv_sem=back_recv.at[h],
            device_id=lister_device(h), device_id_type=MESH,
        )

    def flag(step, stride):
        lane = strides.index(stride)
        return pltpu.make_async_remote_copy(
            src_ref=flag_out.at[step], dst_ref=flag_in.at[lane],
            send_sem=flag_send.at[lane], recv_sem=flag_recv.at[lane],
            device_id=device(stride // n_local, stride % n_local), device_id_type=MESH,
        )

    pl.semaphore_wait(barrier, len(friends))
    others = [(OWN + place) % SHARDS for place in range(1, SHARDS)]
    for h in others:
        names_of(h).start()
    for h in others:
        message(h).start()
    for stride in rounds[0]:
        flag(0, stride).start()

    to_partners[...] = jnp.zeros_like(to_partners)
    to_owners[...] = jnp.zeros_like(to_owners)
    msg[OWN] = out_msg[OWN]
    meta[OWN] = out_meta[OWN]

    def gather(shards_here):
        rows = len(shards_here) * SEATS
        seats = jnp.concatenate([meta[h] for h in shards_here], axis=0)
        wanted = (seats == lax.broadcasted_iota(I32, (rows, LANES), 1)).astype(F32).astype(BF16)
        for place, h in enumerate(shards_here):
            named[h] = wanted[place * SEATS : (place + 1) * SEATS].astype(F32)
        for row in range(ROWS):
            plane = picked(wanted[:, :n_leaf], leaves[pl.ds(row, n_leaf, stride=ROWS), :])
            for place, h in enumerate(shards_here):
                partners[h, row * SEATS : (row + 1) * SEATS, :] = plane[place * SEATS : (place + 1) * SEATS, :]

    def prepare(h):
        firsts[...] = msg[h]
        seconds[...] = partners[h]

    def prepare_slot(slot):
        seat_rows = pl.ds(slot, ROWS, stride=SEATS)
        stages[slot].prepare(firsts[seat_rows, :], seconds[seat_rows, :])

    def finish_slot(slot):
        seat_rows = pl.ds(slot, ROWS, stride=SEATS)
        to_partners[seat_rows, :], to_owners[seat_rows, :] = stages[slot].sums()

    def finish(h):
        on_partner[h] = to_partners[...]
        on_owner[h] = to_owners[...]

    turned = (here_local == 0) * 2 + (here_local == 1) * 1
    turned = turned + (here_local == n_local - 1) * 3 + (here_local == n_local - 2) * 4
    own_turn = 2 * ((7 - turned) % 5)

    def shard_at(place):
        turn = place + (place >= own_turn) * 1
        return turn % 2 * 5 + 4 - (turn // 2 + turned) % 5

    gather([OWN])
    prepare(OWN)
    for slot in range(SLOTS):
        prepare_slot(slot)
    for slot in range(SLOTS):
        stages[slot].strengths()

    def gather_places(group):
        met_here = [shard_at(jnp.int32(place)) for place in group]
        for h in met_here:
            names_of(h).wait_recv()
        gather(met_here)

    groups = ((0, 1, 2), (3, 4, 5), (6, 7, 8))
    gather_places(groups[0])
    first_shard = shard_at(jnp.int32(0))
    message(first_shard).wait_recv()
    prepare(first_shard)
    for slot in range(SLOTS):
        prepare_slot(slot)

    def turn(place, h_before):
        h = shard_at(place - 1)
        h_next = shard_at(jnp.minimum(place, SHARDS - 2))

        @pl.when(place < SHARDS - 1)
        def _():
            message(h_next).wait_recv()

        for group in groups[1:]:

            @pl.when(place == group[0])
            def _(group=group):
                gather_places(group)

        for step, each in enumerate(rounds):

            @pl.when(place == SHARDS - 1 - 2 * (len(rounds) - 1 - step))
            def _(step=step, each=each):
                heard = flag_out[step]
                for stride in each:
                    flag(step, stride).wait()
                    heard = jnp.maximum(heard, flag_in[strides.index(stride)])
                flag_out[step + 1] = heard
                if step + 1 < len(rounds):
                    for stride in rounds[step + 1]:
                        flag(step + 1, stride).start()

        prepare(h_next)
        for slot in range(SLOTS):
            finish_slot(slot)
            stages[slot].strengths()
            prepare_slot(slot)
        finish(h_before)

        @pl.when(place >= 2)
        def _():
            answer(h_before).start()

        return h

    h_end = lax.fori_loop(1, SHARDS, turn, jnp.int32(OWN))
    for slot in range(SLOTS):
        finish_slot(slot)
    finish(h_end)
    answer(h_end).start()
    over[...] = flag_out[len(rounds)]
    for h in others:
        names_of(h).wait_send()
        message(h).wait_send()

    def planes(sources):
        for half in range(2):
            for c in range(3):
                rows = slice((half * 4 + c) * SEATS, (half * 4 + c + 1) * SEATS)
                yield c, slice(half * LANES, (half + 1) * LANES), jnp.concatenate(
                    [source[h, rows, :] for h, source in enumerate(sources)], axis=0
                )

    wanted = jnp.concatenate([named[h] for h in range(SHARDS)], axis=0).astype(BF16)[:, :n_leaf]
    met = lax.dot_general(kept, wanted, last, preferred_element_type=F32).astype(BF16)
    for c, lanes, forces_met in planes([on_partner] * SHARDS):
        total[c, :, lanes] = picked(met, forces_met)
    for h in others:
        answer(h).wait()
    for c, lanes, forces_listed in planes([on_owner if h == OWN else landed for h in range(SHARDS)]):
        total[c, :, lanes] = total[c, :, lanes] + picked(back, forces_listed)


def forces(leaves, pairs, count, active, n_region, n_local):
    vmem = pl.BlockSpec(memory_space=pltpu.VMEM)
    n_leaf = leaves.shape[0] // ROWS
    rounds = flag_rounds(n_region * n_local)
    n_flag = sum(len(each) for each in rounds)
    message = pltpu.VMEM((SHARDS, ROWS * SEATS, LANES), F32)
    names = pltpu.VMEM((SHARDS, SEATS, LANES), I32)

    def kernel(*refs):
        forces_kernel(n_region, n_local, *refs)

    return pl.pallas_call(
        kernel,
        out_shape=(
            jax.ShapeDtypeStruct((3, n_leaf, WIDTH), F32),
            jax.ShapeDtypeStruct((8, LANES), I32),
        ),
        in_specs=[vmem, vmem, vmem, vmem],
        out_specs=(vmem, vmem),
        scratch_shapes=[
            message,
            names,
            message,
            names,
            message,
            pltpu.VMEM((SHARDS, SEATS, LANES), F32),
            message,
            message,
            message,
            pltpu.VMEM((len(rounds) + 1, 8, LANES), I32),
            pltpu.VMEM((n_flag, 8, LANES), I32),
        ]
        + [pltpu.VMEM((ROWS * SEATS, LANES), F32)] * 4
        + [pltpu.SemaphoreType.DMA((SHARDS,))] * 6
        + [pltpu.SemaphoreType.DMA((n_flag,))] * 2
        + [pltpu.VMEM(*shape) for shape in Stage.shapes] * SLOTS,
        compiler_params=pltpu.CompilerParams(
            collective_id=0, has_side_effects=True, vmem_limit_bytes=32 * 2**20
        ),
        name="forces",
    )(leaves, pairs, count, active)


def passed_along(value, axis, steps):
    if steps == 0:
        return value
    count = lax.axis_size(axis)
    pairs = [(source, (source + steps) % count) for source in range(count)]
    return lax.ppermute(value, axis, pairs)


def dense_pair(first, second):
    dx = second[:3, None, :] - first[:3, :, None]
    r2 = jnp.sum(dx * dx, axis=0) + 0.09
    dist = jnp.sqrt(r2)
    kern = (lax.erfc(dist * 0.5) + dist * INV_SQRT_PI * jnp.exp(-r2 * 0.25)) / (r2 * dist)
    weighted = dx * kern[None, :, :]
    on_first = jnp.sum(weighted * second[3][None, None, :], axis=2)
    on_second = -jnp.sum(weighted * first[3][None, :, None], axis=1)
    return (on_first, on_second)


def by_windows(positions, pair_list, pair_count):
    leaf_dev, _, width = positions.shape
    offsets = (-2, -1, 0, 1, 2)
    here = jnp.concatenate([passed_along(positions, "local", -offset) for offset in offsets], axis=0)
    table = jnp.concatenate([here, passed_along(here, "region", -1)], axis=0)
    span = here.shape[0]
    slots = pair_list.shape[0]
    alive = (jnp.arange(slots, dtype=I32) < pair_count[0]).astype(F32)

    def step(carry, inputs):
        own_part, react_part = carry
        pair, weight = inputs
        on_first, on_second = dense_pair(positions[pair[0]], table[pair[1]])
        own_part = own_part.at[pair[0]].add(on_first * weight)
        react_part = react_part.at[pair[1]].add(on_second * weight)
        return ((own_part, react_part), None)

    own_part = jnp.zeros((leaf_dev, 3, width), F32)
    reaction = jnp.zeros((2 * span, 3, width), F32)
    (own_part, reaction), _ = lax.scan(step, (own_part, reaction), (pair_list, alive))
    reaction = reaction[:span] + passed_along(reaction[span:], "region", 1)
    for place, offset in enumerate(offsets):
        piece = reaction[place * leaf_dev : (place + 1) * leaf_dev]
        own_part = own_part + passed_along(piece, "local", offset)
    return own_part.transpose(1, 0, 2)


def shards(positions, pair_list, pair_count, active):
    n_region = lax.axis_size("region")
    n_local = lax.axis_size("local")
    n_leaf, n_row, width = positions.shape
    leaves = positions.reshape(n_leaf, n_row, 2, LANES).transpose(0, 2, 1, 3).reshape(n_leaf * ROWS, LANES)
    total, over = forces(
        leaves, pair_list.T, pair_count.reshape(1, 1), active.reshape(1, n_leaf), n_region, n_local
    )
    total = lax.cond(
        over[0, 0] > 0,
        lambda total: by_windows(positions, pair_list, pair_count) * active.astype(F32)[None, :, None],
        lambda total: total,
        total,
    )
    return total.transpose(1, 0, 2)


def solution(mesh):
    return jax.shard_map(
        shards,
        mesh=mesh,
        in_specs=(
            P(("region", "local"), None, None),
            P(("region", "local"), None),
            P(("region", "local")),
            P(("region", "local")),
        ),
        out_specs=P(("region", "local"), None, None),
        check_vma=False,
    )
```
